32 devices in a mesh: col: 8 (over z, x), row: 4 (over y, core).
Axes of the slice: x: 2, y: 2, z: 4, core: 2. Of those that a mesh axis runs over, the one named last changes fastest.
Arguments:
- tiles: bfloat16 [4, 8, 8, 1024, 512], P('row', 'col'), may hold values from -0.15625 to 0.15625
- tile_index: int32 [4, 8, 8, 2], P('row', 'col'), may hold values from 0 to 15, as said below
- tile_count: int32 [4, 8], P('row', 'col'), may hold values from 1 to 8, as said below
- weights: float32 [32], replicated, may hold values from 0.02 to 0.98
- carbon: float32 [8, 8192], P('col', 'row'), may hold values from 0.1 to 2
- completion: float32 [8, 8192], P('col', 'row'), may hold values from 0.1 to 2
- demand: float32 [4, 16384], P('row', 'col'), may hold values from -6 to 6
- row_kind: int32 [4, 16384], P('row', 'col'), may hold values 0 or 1
- primal_start: float32 [32, 8, 8192], P(None, 'col', 'row'), may hold values from 0 to 2
- dual_start: float32 [32, 4, 16384], P(None, 'row', 'col'), may hold values from -6 to 6
Outputs:
- primal_out: float32 [32, 8, 8192], P(None, 'col', 'row')
- dual_out: float32 [32, 4, 16384], P(None, 'row', 'col')
The draws below stay inside these ranges and needn't reach their ends.
Inputs may be any that keep to these rules, and one draw needn't show every extreme that they name: `tile_index`: column 0 is a local block row below 16, column 1 a local block column below 16; the pairs of one region pair are all different. `tile_count`: at least one region pair holds 8 live tiles in every draw.
All inputs are finite; a program needn't handle non-finite values. No bound on the sum of `row_kind` on one device may be relied on, other than what follows from the above.
Results may differ from the reference program's by a relative error of at most 0.0021.
Values may be sent and summed in bfloat16 or wider, within the bound.
No kernel may reach another device: no remote copies, remote signals or barrier semaphores. Data moves between devices by JAX's collectives and lax.ppermute only.
A program may use at most 64 MiB of HBM per device.

```python
import math
import jax
import jax.numpy as jnp
from jax import lax

K = 32
TR = 1024
TC = 512
BR_DEV = 16
BC_DEV = 16
TMAX = 8
ITERS = 2
ROW_REGIONS = 4
COL_REGIONS = 8
ROWS_REG = 16384
COLS_REG = 8192


def draw_tile_count(key, part):
    first, second = jax.random.split(jax.random.fold_in(key, 11))
    pairs = ROW_REGIONS * COL_REGIONS
    counts = jax.random.randint(first, (pairs,), 1, TMAX // 2 + 1, dtype=jnp.int32)
    busiest = jax.random.randint(second, (), 0, pairs, dtype=jnp.int32)
    counts = jnp.where(jnp.arange(pairs, dtype=jnp.int32) == busiest, TMAX, counts)
    return counts.astype(jnp.int32).reshape(ROW_REGIONS, COL_REGIONS)


def draw_tile_index(key, part):
    pairs = ROW_REGIONS * COL_REGIONS
    keys = jax.random.split(jax.random.fold_in(key, 23), pairs)

    def one_pair(single):
        order = jax.random.permutation(single, BR_DEV * BC_DEV)[:TMAX]
        return jnp.stack([order // BC_DEV, order % BC_DEV], axis=1)
    picked = jax.vmap(one_pair)(keys)
    return picked.astype(jnp.int32).reshape(ROW_REGIONS, COL_REGIONS, TMAX, 2)


def place_ends(array, rng, smallest, high):
    longest = array.shape.index(max(array.shape))
    spots = []
    for shift in (0, 1):
        where = [jax.random.randint(jax.random.fold_in(rng, axis), (), 0, length) for axis, length in enumerate(array.shape)]
        where[longest] = (where[longest] + shift) % array.shape[longest]
        spots.append(tuple(where))
    return array.at[spots[0]].set(smallest).at[spots[1]].set(high)


def shard_levels(rng, extent, cuts, least, top_value):
    loudness = 1.0
    for position, blocks in cuts:
        draws = jax.random.uniform(jax.random.fold_in(jax.random.fold_in(rng, 6), position), (blocks,), jnp.float32, least / len(cuts), top_value / len(cuts))
        loudness = loudness * jnp.repeat(jnp.exp(draws), extent[position] // blocks).reshape((-1,) + (1,) * (len(extent) - 1 - position))
    return loudness


def normal_values(key, dims, spread, bound, pieces=(), held_as=jnp.bfloat16):
    gain = shard_levels(key, dims, pieces, -0.22, 0.18) if pieces else 1.0
    drawn = jax.random.normal(key, dims, jnp.float32) * spread * gain
    return jnp.minimum(jnp.maximum(drawn, -bound), bound).astype(held_as)


def setup_inputs(seed: int = 0) -> dict:
    key_of = jax.random.split(jax.random.key(seed), 11)
    return {
        "tiles": normal_values(key_of[0], (ROW_REGIONS, COL_REGIONS, TMAX, TR, TC), (3 * TC) ** -0.5, 0.15625, ((0, 4), (1, 8))),
        "tile_index": draw_tile_index(jax.random.fold_in(key_of[10], 71), 0),
        "tile_count": draw_tile_count(jax.random.fold_in(key_of[10], 71), 0),
        "weights": jnp.clip(jax.random.uniform(key_of[3], (K,), jnp.float32, 0.02, 0.98), 0.02, 0.98),
        "carbon": jnp.clip(jnp.exp(math.log(2.0) - 2.9957323 * jax.random.uniform(key_of[4], (COL_REGIONS, COLS_REG), jnp.float32) ** shard_levels(key_of[4], (COL_REGIONS, COLS_REG), ((0, 8), (1, 4)), -0.2, 0.2)), 0.1, 2.0),
        "completion": jnp.clip(jnp.exp(math.log(2.0) - 2.9957323 * jax.random.uniform(key_of[5], (COL_REGIONS, COLS_REG), jnp.float32) ** shard_levels(key_of[5], (COL_REGIONS, COLS_REG), ((0, 8), (1, 4)), -0.2, 0.2)), 0.1, 2.0),
        "demand": normal_values(key_of[6], (ROW_REGIONS, ROWS_REG), 1.0, 6.0, ((0, 4), (1, 8)), jnp.float32),
        "row_kind": place_ends((jax.random.randint(key_of[7], (ROW_REGIONS, ROWS_REG), 0, 2) < 1).astype(jnp.int32), jax.random.fold_in(key_of[7], 1), 0, 1),
        "primal_start": jnp.clip(2.0 * jax.random.uniform(key_of[8], (K, COL_REGIONS, COLS_REG), jnp.float32) ** shard_levels(key_of[8], (K, COL_REGIONS, COLS_REG), ((1, 8), (2, 4)), -0.2, 0.2), 0.0, 2.0),
        "dual_start": normal_values(key_of[9], (K, ROW_REGIONS, ROWS_REG), 1.0, 6.0, ((1, 4), (2, 8)), jnp.float32),
    }


step_primal = 0.4
step_dual = 0.4


def reference(tiles, tile_index, tile_count, weights, carbon, completion, demand, row_kind, primal_start, dual_start):
    region_rows = tiles.shape[0]
    region_cols = tiles.shape[1]
    slots = tiles.shape[2]
    rows_tile = tiles.shape[3]
    cols_tile = tiles.shape[4]
    flat = tiles.reshape(-1, rows_tile, cols_tile)
    row_block = (jnp.arange(region_rows, dtype=jnp.int32)[:, None, None] * BR_DEV + tile_index[..., 0]).reshape(-1).astype(jnp.int32)
    col_block = (jnp.arange(region_cols, dtype=jnp.int32)[None, :, None] * BC_DEV + tile_index[..., 1]).reshape(-1).astype(jnp.int32)
    alive = (jnp.arange(slots, dtype=jnp.int32)[None, None, :] < tile_count[:, :, None]).reshape(-1)
    count_all = flat.shape[0]
    width = weights.shape[0]
    total_rows = region_rows * rows_tile * BR_DEV
    total_cols = region_cols * cols_tile * BC_DEV

    def transpose_all(dual_round):
        def visit(index, total):
            def add(current):
                rows_at = (row_block[index] * rows_tile).astype(jnp.int32)
                cols_at = (col_block[index] * cols_tile).astype(jnp.int32)
                piece = lax.dynamic_slice_in_dim(dual_round, rows_at, rows_tile, 1)
                term = jnp.dot(piece, flat[index], preferred_element_type=jnp.float32)
                prior = lax.dynamic_slice_in_dim(current, cols_at, cols_tile, 1)
                return lax.dynamic_update_slice_in_dim(current, prior + term, cols_at, 1)
            return lax.cond(alive[index], add, lambda current: current, total)
        return lax.fori_loop(0, count_all, visit, jnp.zeros((width, total_cols), jnp.float32))

    def forward_all(extra):
        def visit(index, total):
            def add(current):
                rows_at = (row_block[index] * rows_tile).astype(jnp.int32)
                cols_at = (col_block[index] * cols_tile).astype(jnp.int32)
                piece = lax.dynamic_slice_in_dim(extra, cols_at, cols_tile, 1)
                term = jnp.dot(piece, flat[index].T, preferred_element_type=jnp.float32)
                prior = lax.dynamic_slice_in_dim(current, rows_at, rows_tile, 1)
                return lax.dynamic_update_slice_in_dim(current, prior + term, rows_at, 1)
            return lax.cond(alive[index], add, lambda current: current, total)
        return lax.fori_loop(0, count_all, visit, jnp.zeros((width, total_rows), jnp.float32))

    share = weights[:, None]
    cost = share * carbon.reshape(1, -1) + (1.0 - share) * completion.reshape(1, -1)
    bound_rows = demand.reshape(1, -1)
    kind_rows = row_kind.reshape(1, -1)
    primal = primal_start.reshape(width, -1)
    dual = dual_start.reshape(width, -1)
    for step in range(ITERS):
        dual_round = dual.astype(jnp.bfloat16)
        pull = transpose_all(dual_round)
        fresh = jnp.maximum(primal - step_primal * (cost - pull), 0.0)
        extra = (2.0 * fresh - primal).astype(jnp.bfloat16)
        primal = fresh
        push = forward_all(extra)
        moved = dual + step_dual * (bound_rows - push)
        dual = jnp.where(kind_rows == 1, jnp.maximum(moved, 0.0), moved)
    return primal.reshape(primal_start.shape), dual.reshape(dual_start.shape)
```

```python
import functools

import jax
import jax.numpy as jnp
from jax import lax
from jax.experimental import pallas as pl
from jax.experimental.pallas import tpu as pltpu
from jax.sharding import PartitionSpec as P

BR_DEV = 16
BC_DEV = 16
ITERS = 2


step_primal = 0.4
step_dual = 0.4

VMEM_LIMIT = 24 * 1024 * 1024


def sweep_kernel(forward, pieces, outs, per_in, per_out, info, tiles, *refs):
    parts = refs[:pieces]
    results = refs[pieces : pieces + outs]
    held, total, operand, arrived = refs[pieces + outs :]
    slots = tiles.shape[0]
    live = info[2 * slots]
    me_in = info[2 * slots + 1]
    me_out = info[2 * slots + 2]
    span_in = operand.shape[1]
    span_out = total.shape[2]

    def fetch(slot):
        return pltpu.make_async_copy(tiles.at[slot], held.at[slot], arrived.at[slot])

    def start(slot, carry):
        fetch(slot).start()
        return carry

    lax.fori_loop(0, live, start, 0)
    total[...] = jnp.zeros_like(total)

    def visit(slot, carry):
        block_row = info[2 * slot]
        block_col = info[2 * slot + 1]
        block_in = block_col if forward else block_row
        block_out = block_row if forward else block_col
        source = (block_in // per_in) ^ me_in
        place = pl.multiple_of((block_in % per_in) * span_in, span_in)
        for k in range(pieces):

            @pl.when(source == k)
            def _():
                operand[...] = parts[k][:, pl.ds(place, span_in)]

        fetch(slot).wait()
        contract = (((1,), (1,)), ((), ())) if forward else (((1,), (0,)), ((), ()))
        total[block_out] += lax.dot_general(
            operand[...], held[slot], contract, preferred_element_type=jnp.float32
        )
        return carry

    lax.fori_loop(0, live, visit, 0)
    for k in range(outs):
        first = (me_out ^ k) * per_out
        for b in range(per_out):
            results[k][:, b * span_out : (b + 1) * span_out] = total[first + b].astype(
                results[k].dtype
            )


def sweep(forward, tiles, info, parts, outs, per_in, per_out, blocks_out):
    slots, rows_tile, cols_tile = tiles.shape
    width = parts[0].shape[0]
    span_in, span_out = (cols_tile, rows_tile) if forward else (rows_tile, cols_tile)
    pieces = len(parts)
    vmem = pl.BlockSpec(memory_space=pltpu.VMEM)
    return pl.pallas_call(
        functools.partial(sweep_kernel, forward, pieces, outs, per_in, per_out),
        out_shape=[
            jax.ShapeDtypeStruct((width, per_out * span_out), jnp.bfloat16)
        ]
        * outs,
        in_specs=[pl.BlockSpec(memory_space=pltpu.SMEM), pl.BlockSpec(memory_space=pl.ANY)]
        + [vmem] * pieces,
        out_specs=[vmem] * outs,
        scratch_shapes=[
            pltpu.VMEM(tiles.shape, tiles.dtype),
            pltpu.VMEM((blocks_out, width, span_out), jnp.float32),
            pltpu.VMEM((width, span_in), jnp.bfloat16),
            pltpu.SemaphoreType.DMA((slots,)),
        ],
        compiler_params=pltpu.CompilerParams(vmem_limit_bytes=VMEM_LIMIT),
        cost_estimate=pl.CostEstimate(
            flops=2 * slots * width * rows_tile * cols_tile,
            bytes_accessed=tiles.size * 2,
            transcendentals=0,
        ),
        name="forward_sweep" if forward else "transpose_sweep",
    )(info, tiles, *parts)


def swap(value, axis, size, k):
    return lax.ppermute(value, axis, [(i, i ^ k) for i in range(size)])


def gather_pairs(own, axis, size):
    parts = [None] * size
    parts[0] = own
    for k in range(2, size, 2):
        parts[k] = swap(own, axis, size, k)
    for k in range(0, size, 2):
        parts[k + 1] = swap(parts[k], axis, size, 1)
    return parts


def sum_direct(parts, axis, size):
    total = parts[0].astype(jnp.float32)
    for k in range(1, size):
        total = total + swap(parts[k], axis, size, k).astype(jnp.float32)
    return total


def body(
    rows,
    cols,
    tiles,
    tile_index,
    tile_count,
    weights,
    carbon,
    completion,
    demand,
    row_kind,
    primal_start,
    dual_start,
):
    blocks = tiles[0, 0]
    info = jnp.concatenate(
        [
            tile_index.reshape(-1),
            tile_count.reshape(-1),
            lax.axis_index("col")[None],
            lax.axis_index("row")[None],
        ]
    ).astype(jnp.int32)
    info_back = jnp.concatenate([info[:-2], info[-1:], info[-2:-1]])
    primal = primal_start[:, 0, :]
    dual = dual_start[:, 0, :]
    per_row = dual.shape[1] // blocks.shape[1]
    per_col = primal.shape[1] // blocks.shape[2]
    share = weights[:, None]
    cost = share * carbon + (1.0 - share) * completion
    for step in range(ITERS):
        dual_parts = gather_pairs(dual.astype(jnp.bfloat16), "col", cols)
        pull_parts = sweep(
            False, blocks, info, dual_parts, rows, per_row, per_col, BC_DEV
        )
        pull = sum_direct(pull_parts, "row", rows)
        fresh = jnp.maximum(primal - step_primal * (cost - pull), 0.0)
        extra = (2.0 * fresh - primal).astype(jnp.bfloat16)
        primal = fresh
        extra_parts = gather_pairs(extra, "row", rows)
        push_parts = sweep(
            True, blocks, info_back, extra_parts, cols, per_col, per_row, BR_DEV
        )
        push = sum_direct(push_parts, "col", cols)
        moved = dual + step_dual * (demand - push)
        dual = jnp.where(row_kind == 1, jnp.maximum(moved, 0.0), moved)
    return (primal[:, None, :], dual[:, None, :])


def solution(mesh):
    placed = (
        P("row", "col", None, None, None),
        P("row", "col", None, None),
        P("row", "col"),
        P(),
        P("col", "row"),
        P("col", "row"),
        P("row", "col"),
        P("row", "col"),
        P(None, "col", "row"),
        P(None, "row", "col"),
    )
    return jax.shard_map(
        functools.partial(body, mesh.shape["row"], mesh.shape["col"]),
        mesh=mesh,
        in_specs=placed,
        out_specs=(P(None, "col", "row"), P(None, "row", "col")),
        check_vma=False,
    )
```

```python
import functools

import jax
import jax.numpy as jnp
from jax import lax
from jax.experimental import pallas as pl
from jax.experimental.pallas import tpu as pltpu
from jax.sharding import PartitionSpec as P

BR_DEV = 16
BC_DEV = 16
ITERS = 2


step_primal = 0.4
step_dual = 0.4

VMEM_LIMIT = 24 * 1024 * 1024


def sweep_kernel(forward, pieces, outs, per_in, per_out, info, tiles, *refs):
    parts = refs[:pieces]
    results = refs[pieces : pieces + outs]
    held, total, operand, arrived = refs[pieces + outs :]
    slots = tiles.shape[0]
    live = info[2 * slots]
    me_in = info[2 * slots + 1]
    me_out = info[2 * slots + 2]
    span_in = operand.shape[1]
    span_out = total.shape[2]

    def fetch(slot):
        return pltpu.make_async_copy(tiles.at[slot], held.at[slot], arrived.at[slot])

    def start(slot, carry):
        fetch(slot).start()
        return carry

    lax.fori_loop(0, live, start, 0)
    total[...] = jnp.zeros_like(total)

    def visit(slot, carry):
        block_row = info[2 * slot]
        block_col = info[2 * slot + 1]
        block_in = block_col if forward else block_row
        block_out = block_row if forward else block_col
        source = (block_in // per_in) ^ me_in
        place = pl.multiple_of((block_in % per_in) * span_in, span_in)
        for k in range(pieces):

            @pl.when(source == k)
            def _():
                operand[...] = parts[k][:, pl.ds(place, span_in)]

        fetch(slot).wait()
        contract = (((1,), (1,)), ((), ())) if forward else (((1,), (0,)), ((), ()))
        total[block_out] += lax.dot_general(
            operand[...], held[slot], contract, preferred_element_type=jnp.float32
        )
        return carry

    lax.fori_loop(0, live, visit, 0)
    for k in range(outs):
        first = (me_out ^ k) * per_out
        for b in range(per_out):
            results[k][:, b * span_out : (b + 1) * span_out] = total[first + b].astype(
                results[k].dtype
            )


def sweep(forward, tiles, info, parts, kinds, per_in, per_out, blocks_out):
    slots, rows_tile, cols_tile = tiles.shape
    width = parts[0].shape[0]
    span_in, span_out = (cols_tile, rows_tile) if forward else (rows_tile, cols_tile)
    pieces = len(parts)
    outs = len(kinds)
    vmem = pl.BlockSpec(memory_space=pltpu.VMEM)
    return pl.pallas_call(
        functools.partial(sweep_kernel, forward, pieces, outs, per_in, per_out),
        out_shape=[
            jax.ShapeDtypeStruct((width, per_out * span_out), kind) for kind in kinds
        ],
        in_specs=[pl.BlockSpec(memory_space=pltpu.SMEM), pl.BlockSpec(memory_space=pltpu.HBM)]
        + [vmem] * pieces,
        out_specs=[vmem] * outs,
        scratch_shapes=[
            pltpu.VMEM(tiles.shape, tiles.dtype),
            pltpu.VMEM((blocks_out, width, span_out), jnp.float32),
            pltpu.VMEM((width, span_in), jnp.bfloat16),
            pltpu.SemaphoreType.DMA((slots,)),
        ],
        compiler_params=pltpu.CompilerParams(vmem_limit_bytes=VMEM_LIMIT),
        cost_estimate=pl.CostEstimate(
            flops=2 * slots * width * rows_tile * cols_tile,
            bytes_accessed=tiles.size * 2,
            transcendentals=0,
        ),
        name="forward_sweep" if forward else "transpose_sweep",
    )(info, tiles, *parts)


def swap(value, axis, size, k):
    return lax.ppermute(value, axis, [(i, i ^ k) for i in range(size)])


def gather_pairs(own, axis, size):
    parts = [None] * size
    parts[0] = own
    for k in range(2, size, 2):
        parts[k] = swap(own, axis, size, k)
    for k in range(0, size, 2):
        parts[k + 1] = swap(parts[k], axis, size, 1)
    return parts


def sum_pairs(parts, axis, size):
    total = None
    for k in range(size - 2, -1, -2):
        pair = parts[k] + swap(parts[k + 1], axis, size, 1).astype(jnp.float32)
        if k:
            pair = swap(pair.astype(jnp.bfloat16), axis, size, k).astype(jnp.float32)
        total = pair if total is None else total + pair
    return total


def sum_direct(parts, axis, size):
    total = parts[0].astype(jnp.float32)
    for k in range(1, size):
        total = total + swap(parts[k], axis, size, k).astype(jnp.float32)
    return total


def body(
    rows,
    cols,
    tiles,
    tile_index,
    tile_count,
    weights,
    carbon,
    completion,
    demand,
    row_kind,
    primal_start,
    dual_start,
):
    blocks = tiles[0, 0]
    info = jnp.concatenate(
        [
            tile_index.reshape(-1),
            tile_count.reshape(-1),
            lax.axis_index("col")[None],
            lax.axis_index("row")[None],
        ]
    ).astype(jnp.int32)
    info_back = jnp.concatenate([info[:-2], info[-1:], info[-2:-1]])
    primal = primal_start[:, 0, :]
    dual = dual_start[:, 0, :]
    per_row = dual.shape[1] // blocks.shape[1]
    per_col = primal.shape[1] // blocks.shape[2]
    share = weights[:, None]
    pull_kinds = [jnp.float32] + [jnp.bfloat16] * (rows - 1)
    push_kinds = [jnp.float32, jnp.bfloat16] * (cols // 2)
    cost = share * carbon + (1.0 - share) * completion
    for step in range(ITERS):
        dual_parts = gather_pairs(dual.astype(jnp.bfloat16), "col", cols)
        pull_parts = sweep(
            False, blocks, info, dual_parts, pull_kinds, per_row, per_col, BC_DEV
        )
        pull = sum_direct(pull_parts, "row", rows)
        fresh = jnp.maximum(primal - step_primal * (cost - pull), 0.0)
        extra = (2.0 * fresh - primal).astype(jnp.bfloat16)
        primal = fresh
        extra_parts = gather_pairs(extra, "row", rows)
        push_parts = sweep(
            True, blocks, info_back, extra_parts, push_kinds, per_col, per_row, BR_DEV
        )
        push = sum_pairs(push_parts, "col", cols)
        moved = dual + step_dual * (demand - push)
        dual = jnp.where(row_kind == 1, jnp.maximum(moved, 0.0), moved)
    return (primal[:, None, :], dual[:, None, :])


def solution(mesh):
    placed = (
        P("row", "col", None, None, None),
        P("row", "col", None, None),
        P("row", "col"),
        P(),
        P("col", "row"),
        P("col", "row"),
        P("row", "col"),
        P("row", "col"),
        P(None, "col", "row"),
        P(None, "row", "col"),
    )
    return jax.shard_map(
        functools.partial(body, mesh.shape["row"], mesh.shape["col"]),
        mesh=mesh,
        in_specs=placed,
        out_specs=(P(None, "col", "row"), P(None, "row", "col")),
        check_vma=False,
    )
```

```python
import functools

import jax
import jax.numpy as jnp
from jax import lax
from jax.experimental import pallas as pl
from jax.experimental.pallas import tpu as pltpu
from jax.sharding import PartitionSpec as P

BR_DEV = 16
BC_DEV = 16
ITERS = 2


step_primal = 0.4
step_dual = 0.4

VMEM_LIMIT = 24 * 1024 * 1024
FETCH_LIMIT = 46 * 1024 * 1024


def sweep_kernel(forward, fetched, pieces, outs, per_in, per_out, info, tiles, *refs):
    parts = refs[:pieces][::-1]
    results = refs[pieces : pieces + outs]
    total, operand = refs[pieces + outs : pieces + outs + 2]
    slots = tiles.shape[0]
    live = info[2 * slots]
    me_in = info[2 * slots + 1]
    me_out = info[2 * slots + 2]
    span_in = operand.shape[1]
    span_out = total.shape[2]
    held = tiles
    if fetched:
        held, arrived = refs[pieces + outs + 2 :]

        def fetch(slot):
            return pltpu.make_async_copy(tiles.at[slot], held.at[slot], arrived.at[slot])

        def start(slot, carry):
            fetch(slot).start()
            return carry

        lax.fori_loop(0, live, start, 0)
    total[...] = jnp.zeros_like(total)

    def visit(slot, carry):
        block_row = info[2 * slot]
        block_col = info[2 * slot + 1]
        block_in = block_col if forward else block_row
        block_out = block_row if forward else block_col
        source = (block_in // per_in) ^ me_in
        place = pl.multiple_of((block_in % per_in) * span_in, span_in)
        for k in range(pieces):

            @pl.when(source == k)
            def _():
                operand[...] = parts[k][:, pl.ds(place, span_in)]

        if fetched:
            fetch(slot).wait()
        contract = (((1,), (1,)), ((), ())) if forward else (((1,), (0,)), ((), ()))
        total[block_out] += lax.dot_general(
            operand[...], held[slot], contract, preferred_element_type=jnp.float32
        )
        return carry

    lax.fori_loop(0, live, visit, 0)
    for k in range(outs):
        first = (me_out ^ k) * per_out
        for b in range(per_out):
            results[k][:, b * span_out : (b + 1) * span_out] = total[first + b].astype(
                results[k].dtype
            )


def sweep(forward, fetched, tiles, info, parts, kinds, per_in, per_out, blocks_out):
    slots, rows_tile, cols_tile = tiles.shape
    width = parts[0].shape[0]
    span_in, span_out = (cols_tile, rows_tile) if forward else (rows_tile, cols_tile)
    pieces = len(parts)
    outs = len(kinds)
    vmem = pl.BlockSpec(memory_space=pltpu.VMEM)
    scratch = [
        pltpu.VMEM((blocks_out, width, span_out), jnp.float32),
        pltpu.VMEM((width, span_in), jnp.bfloat16),
    ]
    if fetched:
        scratch += [pltpu.VMEM(tiles.shape, tiles.dtype), pltpu.SemaphoreType.DMA((slots,))]
    return pl.pallas_call(
        functools.partial(sweep_kernel, forward, fetched, pieces, outs, per_in, per_out),
        out_shape=[
            jax.ShapeDtypeStruct((width, per_out * span_out), kind) for kind in kinds
        ],
        in_specs=[
            pl.BlockSpec(memory_space=pltpu.SMEM),
            pl.BlockSpec(memory_space=pl.ANY) if fetched else vmem,
        ]
        + [vmem] * pieces,
        out_specs=[vmem] * outs,
        scratch_shapes=scratch,
        compiler_params=pltpu.CompilerParams(
            vmem_limit_bytes=FETCH_LIMIT if fetched else VMEM_LIMIT
        ),
        cost_estimate=pl.CostEstimate(
            flops=2 * slots * width * rows_tile * cols_tile,
            bytes_accessed=tiles.size * 2,
            transcendentals=0,
        ),
        name="forward_sweep" if forward else "transpose_sweep",
    )(info, tiles, *parts[::-1])


def swap(value, axis, size, k):
    return lax.ppermute(value, axis, [(i, i ^ k) for i in range(size)])


def gather_pairs(own, axis, size):
    parts = [None] * size
    parts[0] = own
    for k in range(size - 2, 0, -2):
        parts[k] = swap(own, axis, size, k)
    for k in range(size - 2, -1, -2):
        parts[k + 1] = swap(parts[k], axis, size, 1)
    return parts


def sum_pairs(parts, axis, size):
    total = None
    for k in range(size - 2, -1, -2):
        pair = parts[k] + swap(parts[k + 1], axis, size, 1).astype(jnp.float32)
        if k:
            pair = swap(pair.astype(jnp.bfloat16), axis, size, k).astype(jnp.float32)
        total = pair if total is None else total + pair
    return total


def sum_direct(parts, axis, size):
    total = parts[0].astype(jnp.float32)
    for k in range(1, size):
        total = total + swap(parts[k], axis, size, k).astype(jnp.float32)
    return total


def body(
    rows,
    cols,
    tiles,
    tile_index,
    tile_count,
    weights,
    carbon,
    completion,
    demand,
    row_kind,
    primal_start,
    dual_start,
):
    blocks = tiles[0, 0]
    info = jnp.concatenate(
        [
            tile_index.reshape(-1),
            tile_count.reshape(-1),
            lax.axis_index("col")[None],
            lax.axis_index("row")[None],
        ]
    ).astype(jnp.int32)
    info_back = jnp.concatenate([info[:-2], info[-1:], info[-2:-1]])
    primal = primal_start[:, 0, :]
    dual = dual_start[:, 0, :]
    per_row = dual.shape[1] // blocks.shape[1]
    per_col = primal.shape[1] // blocks.shape[2]
    share = weights[:, None]
    pull_kinds = [jnp.float32] + [jnp.bfloat16] * (rows - 1)
    push_kinds = [jnp.float32, jnp.bfloat16] * (cols // 2)
    cost = share * carbon + (1.0 - share) * completion
    for step in range(ITERS):
        dual_parts = gather_pairs(dual.astype(jnp.bfloat16), "col", cols)
        pull_parts = sweep(
            False, step == 0, blocks, info, dual_parts, pull_kinds, per_row, per_col, BC_DEV
        )
        pull = sum_direct(pull_parts, "row", rows)
        fresh = jnp.maximum(primal - step_primal * (cost - pull), 0.0)
        extra = (2.0 * fresh - primal).astype(jnp.bfloat16)
        primal = fresh
        extra_parts = gather_pairs(extra, "row", rows)
        push_parts = sweep(
            True, False, blocks, info_back, extra_parts, push_kinds, per_col, per_row, BR_DEV
        )
        push = sum_pairs(push_parts, "col", cols)
        moved = dual + step_dual * (demand - push)
        dual = jnp.where(row_kind == 1, jnp.maximum(moved, 0.0), moved)
    return (primal[:, None, :], dual[:, None, :])


def solution(mesh):
    placed = (
        P("row", "col", None, None, None),
        P("row", "col", None, None),
        P("row", "col"),
        P(),
        P("col", "row"),
        P("col", "row"),
        P("row", "col"),
        P("row", "col"),
        P(None, "col", "row"),
        P(None, "row", "col"),
    )
    return jax.shard_map(
        functools.partial(body, mesh.shape["row"], mesh.shape["col"]),
        mesh=mesh,
        in_specs=placed,
        out_specs=(P(None, "col", "row"), P(None, "row", "col")),
        check_vma=False,
    )
```

```python
import functools

import jax
import jax.numpy as jnp
from jax import lax
from jax.experimental import pallas as pl
from jax.experimental.pallas import tpu as pltpu
from jax.sharding import PartitionSpec as P

BR_DEV = 16
BC_DEV = 16
ITERS = 2


step_primal = 0.4
step_dual = 0.4

VMEM_LIMIT = 24 * 1024 * 1024
FETCH_LIMIT = 46 * 1024 * 1024


def sweep_kernel(forward, fetched, parities, pieces, per_in, info, tiles, *refs):
    parts = refs[:pieces][::-1]
    own = 4 if fetched else 2
    results = refs[pieces:-own]
    scratch = refs[-own:]
    total, operand = scratch[:2]
    slots = tiles.shape[0]
    live = info[2 * slots]
    me_in = info[2 * slots + 1]
    me_out = info[2 * slots + 2]
    span_in = operand.shape[1]
    count, width, span_out = total.shape[1:]
    places = [[] for _ in parities]
    per_parity = len(results) // len(parities)
    for p in range(len(parities)):
        for ref in results[p * per_parity : (p + 1) * per_parity]:
            places[p] += [ref.at[h] for h in range(ref.shape[0])]
    per_out = count // len(places[0])
    held = tiles
    if fetched:
        held, arrived = scratch[2:]

        def fetch(slot):
            return pltpu.make_async_copy(tiles.at[slot], held.at[slot], arrived.at[slot])

        def start(slot, carry):
            fetch(slot).start()
            return carry

        lax.fori_loop(0, live, start, 0)
    total[...] = jnp.zeros_like(total)

    def visit(slot, carry):
        block_row = info[2 * slot]
        block_col = info[2 * slot + 1]
        block_in = block_col if forward else block_row
        block_out = block_row if forward else block_col
        target = (block_out // per_out) ^ me_out

        def add():
            source = (block_in // per_in) ^ me_in
            place = pl.multiple_of((block_in % per_in) * span_in, span_in)
            for k in range(pieces):

                @pl.when(source % pieces == k)
                def _():
                    operand[...] = parts[k][source // pieces, :, pl.ds(place, span_in)]

            contract = (((1,), (1,)), ((), ())) if forward else (((1,), (0,)), ((), ()))
            at = (target // 2) * per_out + block_out % per_out
            side = target % 2 if len(parities) == 2 else 0
            total[side, at] += lax.dot_general(
                operand[...], held[slot], contract, preferred_element_type=jnp.float32
            )

        if fetched:
            fetch(slot).wait()
        if len(parities) == 2:
            add()
        else:
            pl.when(target % 2 == parities[0])(add)
        return carry

    lax.fori_loop(0, live, visit, 0)
    for p in range(len(parities)):
        for h, ref in enumerate(places[p]):
            for b in range(per_out):
                ref[:, b * span_out : (b + 1) * span_out] = total[
                    p, h * per_out + b
                ].astype(ref.dtype)


def sweep(forward, fetched, parities, tiles, info, parts, receivers, stacked, blocks_out):
    slots, rows_tile, cols_tile = tiles.shape
    width = parts[0].shape[1]
    span_in, span_out = (cols_tile, rows_tile) if forward else (rows_tile, cols_tile)
    pieces = len(parts)
    half = receivers // 2
    wide = blocks_out // receivers * span_out
    out_shape = []
    for p in parities:
        kind = jnp.bfloat16 if p else jnp.float32
        if stacked:
            out_shape += [jax.ShapeDtypeStruct((half, width, wide), kind)]
        else:
            out_shape += [jax.ShapeDtypeStruct((1, width, wide), kind)] * half
    vmem = pl.BlockSpec(memory_space=pltpu.VMEM)
    scratch = [
        pltpu.VMEM((len(parities), blocks_out // 2, width, span_out), jnp.float32),
        pltpu.VMEM((width, span_in), jnp.bfloat16),
    ]
    if fetched:
        scratch += [pltpu.VMEM(tiles.shape, tiles.dtype), pltpu.SemaphoreType.DMA((slots,))]
    results = pl.pallas_call(
        functools.partial(
            sweep_kernel, forward, fetched, parities, pieces, parts[0].shape[2] // span_in
        ),
        out_shape=out_shape,
        in_specs=[
            pl.BlockSpec(memory_space=pltpu.SMEM),
            pl.BlockSpec(memory_space=pl.ANY) if fetched else vmem,
        ]
        + [vmem] * pieces,
        out_specs=[vmem] * len(out_shape),
        scratch_shapes=scratch,
        compiler_params=pltpu.CompilerParams(
            vmem_limit_bytes=FETCH_LIMIT if fetched else VMEM_LIMIT
        ),
        cost_estimate=pl.CostEstimate(
            flops=len(parities) * slots * width * rows_tile * cols_tile,
            bytes_accessed=tiles.size * len(parities),
            transcendentals=0,
        ),
        name="forward_sweep" if forward else "transpose_sweep",
    )(info, tiles, *parts[::-1])
    each = len(results) // len(parities)
    return [results[i * each : (i + 1) * each] for i in range(len(parities))]


def swap(value, axis, size, k):
    return lax.ppermute(value, axis, [(i, i ^ k) for i in range(size)])


def gather_pairs(own, axis, size):
    parts = [None] * size
    parts[0] = own
    for k in range(size - 2, 0, -2):
        parts[k] = swap(own, axis, size, k)
    for k in range(size - 2, -1, -2):
        parts[k + 1] = swap(parts[k], axis, size, 1)
    return parts


def sum_pairs(kept, sent, axis, size):
    total = None
    for h in range(size // 2 - 1, -1, -1):
        pair = kept[h] + swap(sent[h], axis, size, 1).astype(jnp.float32)
        if h:
            pair = swap(pair.astype(jnp.bfloat16), axis, size, 2 * h).astype(jnp.float32)
        total = pair if total is None else total + pair
    return total


def sum_halves(kept, sent, axis, size):
    here = kept + swap(sent, axis, size, 1).astype(jnp.float32)
    away = here.astype(jnp.bfloat16)
    total = here
    for t in range(1, size // 2):
        other = swap(away, axis, size, 2 * t)
        order = [h ^ t for h in range(size // 2)]
        total = total + jnp.stack([other[h] for h in order]).astype(jnp.float32)
    return total


def body(
    rows,
    cols,
    tiles,
    tile_index,
    tile_count,
    weights,
    carbon,
    completion,
    demand,
    row_kind,
    primal_start,
    dual_start,
):
    blocks = tiles[0, 0]
    info = jnp.concatenate(
        [
            tile_index.reshape(-1),
            tile_count.reshape(-1),
            lax.axis_index("col")[None],
            lax.axis_index("row")[None],
        ]
    ).astype(jnp.int32)
    info_back = jnp.concatenate([info[:-2], info[-1:], info[-2:-1]])
    dual = dual_start[:, 0, :]
    state = jnp.concatenate([primal_start[:, 0, :], carbon, completion])
    states = [state] + [swap(state, "row", rows, k) for k in range(2, rows, 2)]
    states = jnp.stack(states)
    width = weights.shape[0]
    primal = states[:, :width]
    share = weights[:, None]
    cost = share * states[:, width : width + 1] + (1.0 - share) * states[:, width + 1 :]
    for step in range(ITERS):
        dual_parts = gather_pairs(dual.astype(jnp.bfloat16)[None], "col", cols)
        (kept,), (sent,) = sweep(
            False, step == 0, (0, 1), blocks, info, dual_parts, rows, True, BC_DEV
        )
        pull = sum_halves(kept, sent, "row", rows)
        fresh = jnp.maximum(primal - step_primal * (cost - pull), 0.0)
        extra = (2.0 * fresh - primal).astype(jnp.bfloat16)
        primal = fresh
        extra_parts = [extra, swap(extra, "row", rows, 1)]
        kept, sent = sweep(
            True, False, (0, 1), blocks, info_back, extra_parts, cols, False, BR_DEV
        )
        push = sum_pairs(kept, sent, "col", cols)[0]
        moved = dual + step_dual * (demand - push)
        dual = jnp.where(row_kind == 1, jnp.maximum(moved, 0.0), moved)
    return (primal[0][:, None, :], dual[:, None, :])


def solution(mesh):
    placed = (
        P("row", "col", None, None, None),
        P("row", "col", None, None),
        P("row", "col"),
        P(),
        P("col", "row"),
        P("col", "row"),
        P("row", "col"),
        P("row", "col"),
        P(None, "col", "row"),
        P(None, "row", "col"),
    )
    return jax.shard_map(
        functools.partial(body, mesh.shape["row"], mesh.shape["col"]),
        mesh=mesh,
        in_specs=placed,
        out_specs=(P(None, "col", "row"), P(None, "row", "col")),
        check_vma=False,
    )
```

```python
import functools

import jax
import jax.numpy as jnp
from jax import lax
from jax.experimental import pallas as pl
from jax.experimental.pallas import tpu as pltpu
from jax.sharding import PartitionSpec as P

BR_DEV = 16
BC_DEV = 16
ITERS = 2


step_primal = 0.4
step_dual = 0.4

VMEM_LIMIT = 24 * 1024 * 1024
FETCH_LIMIT = 46 * 1024 * 1024


def sweep_kernel(forward, fetched, parity, pieces, per_in, info, tiles, *refs):
    parts = refs[:pieces][::-1]
    own = 4 if fetched else 2
    places = [ref.at[h] for ref in refs[pieces:-own] for h in range(ref.shape[0])]
    total, operand = refs[-own : 2 - own or None]
    slots = tiles.shape[0]
    live = info[2 * slots]
    me_in = info[2 * slots + 1]
    me_out = info[2 * slots + 2]
    span_in = operand.shape[1]
    span_out = total.shape[2]
    per_out = total.shape[0] // len(places)
    held = tiles

    def target(slot):
        return (info[2 * slot + (0 if forward else 1)] // per_out) ^ me_out

    if fetched:
        held, arrived = refs[-2:]

        def fetch(slot):
            return pltpu.make_async_copy(tiles.at[slot], held.at[slot], arrived.at[slot])

        def start(slot, carry):
            @pl.when(target(slot) % 2 == parity)
            def _():
                fetch(slot).start()

            return carry

        lax.fori_loop(0, live, start, 0)
    total[...] = jnp.zeros_like(total)

    def visit(slot, carry):
        @pl.when(target(slot) % 2 == parity)
        def _():
            block_in = info[2 * slot + (1 if forward else 0)]
            block_out = info[2 * slot + (0 if forward else 1)]
            source = (block_in // per_in) ^ me_in
            place = pl.multiple_of((block_in % per_in) * span_in, span_in)
            for k in range(pieces):

                @pl.when(source % pieces == k)
                def _():
                    operand[...] = parts[k][source // pieces, :, pl.ds(place, span_in)]

            if fetched:
                fetch(slot).wait()
            contract = (((1,), (1,)), ((), ())) if forward else (((1,), (0,)), ((), ()))
            total[(target(slot) // 2) * per_out + block_out % per_out] += lax.dot_general(
                operand[...], held[slot], contract, preferred_element_type=jnp.float32
            )

        return carry

    lax.fori_loop(0, live, visit, 0)
    for h, place in enumerate(places):
        for b in range(per_out):
            place[:, b * span_out : (b + 1) * span_out] = total[h * per_out + b].astype(
                place.dtype
            )


def sweep(forward, fetched, parity, tiles, info, parts, receivers, stacked, blocks_out):
    slots, rows_tile, cols_tile = tiles.shape
    width = parts[0].shape[1]
    span_in, span_out = (cols_tile, rows_tile) if forward else (rows_tile, cols_tile)
    pieces = len(parts)
    half = receivers // 2
    wide = blocks_out // receivers * span_out
    kind = jnp.bfloat16 if parity else jnp.float32
    if stacked:
        out_shape = [jax.ShapeDtypeStruct((half, width, wide), kind)]
    else:
        out_shape = [jax.ShapeDtypeStruct((1, width, wide), kind)] * half
    vmem = pl.BlockSpec(memory_space=pltpu.VMEM)
    scratch = [
        pltpu.VMEM((blocks_out // 2, width, span_out), jnp.float32),
        pltpu.VMEM((width, span_in), jnp.bfloat16),
    ]
    if fetched:
        scratch += [pltpu.VMEM(tiles.shape, tiles.dtype), pltpu.SemaphoreType.DMA((slots,))]
    return pl.pallas_call(
        functools.partial(
            sweep_kernel, forward, fetched, parity, pieces, parts[0].shape[2] // span_in
        ),
        out_shape=out_shape,
        in_specs=[
            pl.BlockSpec(memory_space=pltpu.SMEM),
            pl.BlockSpec(memory_space=pl.ANY) if fetched else vmem,
        ]
        + [vmem] * pieces,
        out_specs=[vmem] * len(out_shape),
        scratch_shapes=scratch,
        compiler_params=pltpu.CompilerParams(
            vmem_limit_bytes=FETCH_LIMIT if fetched else VMEM_LIMIT
        ),
        cost_estimate=pl.CostEstimate(
            flops=slots * width * rows_tile * cols_tile,
            bytes_accessed=tiles.size,
            transcendentals=0,
        ),
        name="forward_sweep" if forward else "transpose_sweep",
    )(info, tiles, *parts[::-1])


def swap(value, axis, size, k):
    return lax.ppermute(value, axis, [(i, i ^ k) for i in range(size)])


def gather_pairs(own, axis, size):
    parts = [None] * size
    parts[0] = own
    for k in range(size - 2, 0, -2):
        parts[k] = swap(own, axis, size, k)
    for k in range(size - 2, -1, -2):
        parts[k + 1] = swap(parts[k], axis, size, 1)
    return parts


def sum_pairs(kept, sent, axis, size):
    total = None
    for h in range(size // 2 - 1, -1, -1):
        pair = kept[h] + swap(sent[h], axis, size, 1).astype(jnp.float32)
        if h:
            pair = swap(pair.astype(jnp.bfloat16), axis, size, 2 * h).astype(jnp.float32)
        total = pair if total is None else total + pair
    return total


def sum_halves(kept, sent, axis, size):
    here = kept + swap(sent, axis, size, 1).astype(jnp.float32)
    away = here.astype(jnp.bfloat16)
    total = here
    for t in range(1, size // 2):
        other = swap(away, axis, size, 2 * t)
        order = [h ^ t for h in range(size // 2)]
        total = total + jnp.stack([other[h] for h in order]).astype(jnp.float32)
    return total


def body(
    rows,
    cols,
    tiles,
    tile_index,
    tile_count,
    weights,
    carbon,
    completion,
    demand,
    row_kind,
    primal_start,
    dual_start,
):
    blocks = tiles[0, 0]
    info = jnp.concatenate(
        [
            tile_index.reshape(-1),
            tile_count.reshape(-1),
            lax.axis_index("col")[None],
            lax.axis_index("row")[None],
        ]
    ).astype(jnp.int32)
    info_back = jnp.concatenate([info[:-2], info[-1:], info[-2:-1]])
    dual = dual_start[:, 0, :]
    state = jnp.concatenate([primal_start[:, 0, :], carbon, completion])
    states = [state] + [swap(state, "row", rows, k) for k in range(2, rows, 2)]
    states = jnp.stack(states)
    width = weights.shape[0]
    primal = states[:, :width]
    share = weights[:, None]
    cost = share * states[:, width : width + 1] + (1.0 - share) * states[:, width + 1 :]
    for step in range(ITERS):
        dual_parts = gather_pairs(dual.astype(jnp.bfloat16)[None], "col", cols)
        turn = functools.partial(
            sweep, False, step == 0, tiles=blocks, info=info, parts=dual_parts,
            receivers=rows, stacked=True, blocks_out=BC_DEV,
        )
        (sent,) = turn(1)
        (kept,) = turn(0)
        pull = sum_halves(kept, sent, "row", rows)
        fresh = jnp.maximum(primal - step_primal * (cost - pull), 0.0)
        extra = (2.0 * fresh - primal).astype(jnp.bfloat16)
        primal = fresh
        extra_parts = [extra, swap(extra, "row", rows, 1)]
        turn = functools.partial(
            sweep, True, False, tiles=blocks, info=info_back, parts=extra_parts,
            receivers=cols, stacked=False, blocks_out=BR_DEV,
        )
        sent = turn(1)
        kept = turn(0)
        push = sum_pairs(kept, sent, "col", cols)[0]
        moved = dual + step_dual * (demand - push)
        dual = jnp.where(row_kind == 1, jnp.maximum(moved, 0.0), moved)
    return (primal[0][:, None, :], dual[:, None, :])


def solution(mesh):
    placed = (
        P("row", "col", None, None, None),
        P("row", "col", None, None),
        P("row", "col"),
        P(),
        P("col", "row"),
        P("col", "row"),
        P("row", "col"),
        P("row", "col"),
        P(None, "col", "row"),
        P(None, "row", "col"),
    )
    return jax.shard_map(
        functools.partial(body, mesh.shape["row"], mesh.shape["col"]),
        mesh=mesh,
        in_specs=placed,
        out_specs=(P(None, "col", "row"), P(None, "row", "col")),
        check_vma=False,
    )
```

```python
import functools
import typing

import jax
import jax.numpy as jnp
from jax import lax
from jax.experimental import pallas as pl
from jax.experimental.pallas import tpu as pltpu
from jax.sharding import PartitionSpec as P

BR_DEV = 16
BC_DEV = 16
ITERS = 2


step_primal = 0.4
step_dual = 0.4

VMEM_LIMIT = 24 * 1024 * 1024
FETCH_LIMIT = 46 * 1024 * 1024


def sweep_kernel(plan, info, tiles, *refs):
    refs = list(refs)
    parts = [refs.pop(0) for _ in plan.senders]
    begun = [refs.pop(0) for _ in plan.begun]
    results = [[refs.pop(0) for _ in range(out.arrays)] for out in plan.outs]
    operand = refs.pop(0)
    sums = {}
    for out, result in zip(plan.outs, results):
        sums[out.parity] = result[0] if out.direct else refs.pop(0)
    held, arrived = refs if plan.fetched else (tiles, None)
    slots = tiles.shape[0]
    live = info[2 * slots]
    me_in = info[2 * slots + 1]
    me_out = info[2 * slots + 2]
    span_in = operand.shape[1]
    span_out = tiles.shape[1] if plan.forward else tiles.shape[2]
    per_out = next(iter(sums.values())).shape[2] // span_out

    def ends(slot):
        row, col = info[2 * slot], info[2 * slot + 1]
        return (col, row) if plan.forward else (row, col)

    def accepted(slot):
        block_in, block_out = ends(slot)
        return plan.accept((block_in // plan.per_in) ^ me_in, (block_out // per_out) ^ me_out)

    def fetch(slot):
        return pltpu.make_async_copy(tiles.at[slot], held.at[slot], arrived.at[slot])

    if plan.fetched:

        def start(slot, carry):
            @pl.when(accepted(slot))
            def _():
                fetch(slot).start()

            return carry

        lax.fori_loop(0, live, start, 0)
    for p in sums:
        sums[p][...] = begun[p][...] if begun else jnp.zeros_like(sums[p])

    def visit(slot, carry):
        @pl.when(accepted(slot))
        def _():
            block_in, block_out = ends(slot)
            source = (block_in // plan.per_in) ^ me_in
            target = (block_out // per_out) ^ me_out
            place = pl.multiple_of((block_in % plan.per_in) * span_in, span_in)
            for part, ks in zip(parts, plan.senders):

                @pl.when(functools.reduce(jnp.logical_or, [source == k for k in ks]))
                def _():
                    at = source // 2 if len(ks) > 1 else 0
                    operand[...] = part[at, :, pl.ds(place, span_in)]

            if plan.fetched:
                fetch(slot).wait()
            contract = (((1,), (1,)), ((), ())) if plan.forward else (((1,), (0,)), ((), ()))
            term = lax.dot_general(
                operand[...], held[slot], contract, preferred_element_type=jnp.float32
            )
            to = pl.multiple_of((block_out % per_out) * span_out, span_out)
            for p in sums:

                @pl.when(target % 2 == p)
                def _():
                    sums[p][target // 2, :, pl.ds(to, span_out)] += term

        return carry

    lax.fori_loop(0, live, visit, 0)
    for out, result in zip(plan.outs, results):
        if not out.direct:
            each = sums[out.parity].shape[0] // out.arrays
            for i, ref in enumerate(result):
                ref[...] = sums[out.parity][i * each : (i + 1) * each].astype(ref.dtype)


class Out(typing.NamedTuple):
    parity: int
    kind: typing.Any
    arrays: int

    @property
    def direct(self):
        return self.kind == jnp.float32 and self.arrays == 1


class Plan(typing.NamedTuple):
    forward: bool
    fetched: bool
    outs: tuple
    senders: tuple
    accept: typing.Callable
    begun: tuple
    per_in: int


def sweep(plan, tiles, info, parts, begun, half, wide):
    slots, rows_tile, cols_tile = tiles.shape
    width = parts[0].shape[1]
    span_in = cols_tile if plan.forward else rows_tile
    plan = plan._replace(
        begun=tuple(range(len(begun))), per_in=parts[0].shape[2] // span_in
    )
    out_shape = []
    for out in plan.outs:
        shape = (half // out.arrays, width, wide)
        out_shape += [jax.ShapeDtypeStruct(shape, out.kind)] * out.arrays
    vmem = pl.BlockSpec(memory_space=pltpu.VMEM)
    scratch = [pltpu.VMEM((width, span_in), jnp.bfloat16)]
    for out in plan.outs:
        if not out.direct:
            scratch += [pltpu.VMEM((half, width, wide), jnp.float32)]
    if plan.fetched:
        scratch += [pltpu.VMEM(tiles.shape, tiles.dtype), pltpu.SemaphoreType.DMA((slots,))]
    return pl.pallas_call(
        functools.partial(sweep_kernel, plan),
        out_shape=out_shape,
        in_specs=[
            pl.BlockSpec(memory_space=pltpu.SMEM),
            pl.BlockSpec(memory_space=pl.ANY) if plan.fetched else vmem,
        ]
        + [vmem] * (len(parts) + len(begun)),
        out_specs=[vmem] * len(out_shape),
        scratch_shapes=scratch,
        compiler_params=pltpu.CompilerParams(
            vmem_limit_bytes=FETCH_LIMIT if plan.fetched else VMEM_LIMIT
        ),
        cost_estimate=pl.CostEstimate(
            flops=slots * width * rows_tile * cols_tile,
            bytes_accessed=tiles.size,
            transcendentals=0,
        ),
        name="forward_sweep" if plan.forward else "transpose_sweep",
    )(info, tiles, *parts, *begun)


def swap(value, axis, size, k):
    return lax.ppermute(value, axis, [(i, i ^ k) for i in range(size)])


def gather_pairs(own, axis, size):
    parts = [None] * size
    parts[0] = own
    for k in range(size - 2, 0, -2):
        parts[k] = swap(own, axis, size, k)
    for k in range(size - 2, -1, -2):
        parts[k + 1] = swap(parts[k], axis, size, 1)
    return parts


def sum_pairs(kept, sent, axis, size):
    total = None
    for h in range(size // 2 - 1, -1, -1):
        pair = kept[h] + swap(sent[h], axis, size, 1).astype(jnp.float32)
        if h:
            pair = swap(pair.astype(jnp.bfloat16), axis, size, 2 * h).astype(jnp.float32)
        total = pair if total is None else total + pair
    return total


def sum_halves(kept, sent, axis, size):
    here = kept + swap(sent, axis, size, 1).astype(jnp.float32)
    away = here.astype(jnp.bfloat16)
    total = here
    for t in range(1, size // 2):
        other = swap(away, axis, size, 2 * t)
        order = [h ^ t for h in range(size // 2)]
        total = total + jnp.stack([other[h] for h in order]).astype(jnp.float32)
    return total


def body(
    rows,
    cols,
    tiles,
    tile_index,
    tile_count,
    weights,
    carbon,
    completion,
    demand,
    row_kind,
    primal_start,
    dual_start,
):
    blocks = tiles[0, 0]
    info = jnp.concatenate(
        [
            tile_index.reshape(-1),
            tile_count.reshape(-1),
            lax.axis_index("col")[None],
            lax.axis_index("row")[None],
        ]
    ).astype(jnp.int32)
    info_back = jnp.concatenate([info[:-2], info[-1:], info[-2:-1]])
    dual = dual_start[:, 0, :]
    state = jnp.concatenate([primal_start[:, 0, :], carbon, completion])
    states = [state] + [swap(state, "row", rows, k) for k in range(2, rows, 2)]
    states = jnp.stack(states)
    width = weights.shape[0]
    primal = states[:, :width]
    share = weights[:, None]
    cost = share * states[:, width : width + 1] + (1.0 - share) * states[:, width + 1 :]
    late = [k for k in range(5, cols, 2)]
    early = [k for k in range(cols) if k not in late]

    def is_late(source):
        return (source % 2 == 1) & (source > 3)

    whole, rounded = jnp.float32, jnp.bfloat16
    transpose = Plan(False, False, (), (), None, (), 0)
    forward = Plan(
        True, False, (), tuple(tuple(range(p, rows, 2)) for p in (0, 1)), None, (), 0
    )
    for step in range(ITERS):
        dual_parts = gather_pairs(dual.astype(jnp.bfloat16)[None], "col", cols)
        begun = sweep(
            transpose._replace(
                fetched=step == 0,
                outs=(Out(0, whole, 1), Out(1, whole, 1)),
                senders=tuple((k,) for k in early),
                accept=lambda source, target: jnp.logical_not(is_late(source)),
            ),
            blocks, info, [dual_parts[k] for k in early], [], rows // 2, primal.shape[2],
        )
        kept, sent = sweep(
            transpose._replace(
                outs=(Out(0, whole, 1), Out(1, rounded, 1)),
                senders=tuple((k,) for k in late),
                accept=lambda source, target: is_late(source),
            ),
            blocks, info, [dual_parts[k] for k in late], begun, rows // 2, primal.shape[2],
        )
        pull = sum_halves(kept, sent, "row", rows)
        fresh = jnp.maximum(primal - step_primal * (cost - pull), 0.0)
        extra = (2.0 * fresh - primal).astype(jnp.bfloat16)
        primal = fresh
        extra_parts = [extra, swap(extra, "row", rows, 1)]
        sent = sweep(
            forward._replace(
                outs=(Out(1, rounded, cols // 2),),
                accept=lambda source, target: target % 2 == 1,
            ),
            blocks, info_back, extra_parts, [], cols // 2, dual.shape[1],
        )
        kept = sweep(
            forward._replace(
                outs=(Out(0, whole, cols // 2),),
                accept=lambda source, target: target % 2 == 0,
            ),
            blocks, info_back, extra_parts, [], cols // 2, dual.shape[1],
        )
        push = sum_pairs(kept, sent, "col", cols)[0]
        moved = dual + step_dual * (demand - push)
        dual = jnp.where(row_kind == 1, jnp.maximum(moved, 0.0), moved)
    return (primal[0][:, None, :], dual[:, None, :])


def solution(mesh):
    placed = (
        P("row", "col", None, None, None),
        P("row", "col", None, None),
        P("row", "col"),
        P(),
        P("col", "row"),
        P("col", "row"),
        P("row", "col"),
        P("row", "col"),
        P(None, "col", "row"),
        P(None, "row", "col"),
    )
    return jax.shard_map(
        functools.partial(body, mesh.shape["row"], mesh.shape["col"]),
        mesh=mesh,
        in_specs=placed,
        out_specs=(P(None, "col", "row"), P(None, "row", "col")),
        check_vma=False,
    )
```

```python
import functools
import typing

import jax
import jax.numpy as jnp
from jax import lax
from jax.experimental import pallas as pl
from jax.experimental.pallas import tpu as pltpu
from jax.sharding import PartitionSpec as P

BR_DEV = 16
BC_DEV = 16
ITERS = 2


step_primal = 0.4
step_dual = 0.4

VMEM_LIMIT = 24 * 1024 * 1024
FETCH_LIMIT = 46 * 1024 * 1024


def among(value, ks):
    return functools.reduce(jnp.logical_or, [value == k for k in ks])


def position(value, ks):
    at = 0
    for i, k in enumerate(ks[1:]):
        at = jnp.where(value == k, i + 1, at)
    return at


class Out(typing.NamedTuple):
    ks: tuple
    kind: typing.Any
    stacked: bool

    @property
    def direct(self):
        return self.kind == jnp.float32 and self.stacked


class Plan(typing.NamedTuple):
    forward: bool
    fetched: bool
    senders: tuple
    outs: tuple
    begun: bool


def sweep_kernel(plan, per_in, info, tiles, *refs):
    refs = list(refs)
    parts = [refs.pop(0) for _ in plan.senders]
    begun = [refs.pop(0) for _ in plan.outs] if plan.begun else []
    results = [[refs.pop(0) for _ in (out.ks[:1] if out.stacked else out.ks)] for out in plan.outs]
    operand = refs.pop(0)
    sums = [
        result[0] if out.direct else refs.pop(0) for out, result in zip(plan.outs, results)
    ]
    held, arrived = refs if plan.fetched else (tiles, None)
    slots = tiles.shape[0]
    live = info[2 * slots]
    me_in = info[2 * slots + 1]
    me_out = info[2 * slots + 2]
    span_in = operand.shape[1]
    span_out = tiles.shape[1] if plan.forward else tiles.shape[2]
    per_out = sums[0].shape[2] // span_out

    def ends(slot):
        row, col = info[2 * slot], info[2 * slot + 1]
        return (col, row) if plan.forward else (row, col)

    def accepted(slot):
        block_in, block_out = ends(slot)
        source = (block_in // per_in) ^ me_in
        target = (block_out // per_out) ^ me_out
        return among(source, sum(plan.senders, ())) & among(
            target, sum((out.ks for out in plan.outs), ())
        )

    def fetch(slot):
        return pltpu.make_async_copy(tiles.at[slot], held.at[slot], arrived.at[slot])

    if plan.fetched:

        def start(slot, carry):
            @pl.when(accepted(slot))
            def _():
                fetch(slot).start()

            return carry

        lax.fori_loop(0, live, start, 0)
    for i, total in enumerate(sums):
        total[...] = begun[i][...] if begun else jnp.zeros_like(total)

    def visit(slot, carry):
        @pl.when(accepted(slot))
        def _():
            block_in, block_out = ends(slot)
            source = (block_in // per_in) ^ me_in
            target = (block_out // per_out) ^ me_out
            place = pl.multiple_of((block_in % per_in) * span_in, span_in)
            for part, ks in zip(parts, plan.senders):

                @pl.when(among(source, ks))
                def _():
                    operand[...] = part[position(source, ks), :, pl.ds(place, span_in)]

            if plan.fetched:
                fetch(slot).wait()
            contract = (((1,), (1,)), ((), ())) if plan.forward else (((1,), (0,)), ((), ()))
            term = lax.dot_general(
                operand[...], held[slot], contract, preferred_element_type=jnp.float32
            )
            to = pl.multiple_of((block_out % per_out) * span_out, span_out)
            for total, out in zip(sums, plan.outs):

                @pl.when(among(target, out.ks))
                def _():
                    total[position(target, out.ks), :, pl.ds(to, span_out)] += term

        return carry

    lax.fori_loop(0, live, visit, 0)
    for out, result, total in zip(plan.outs, results, sums):
        if not out.direct:
            each = len(out.ks) // len(result)
            for i, ref in enumerate(result):
                ref[...] = total[i * each : (i + 1) * each].astype(ref.dtype)


def sweep(plan, tiles, info, parts, begun, wide):
    slots, rows_tile, cols_tile = tiles.shape
    width = parts[0].shape[1]
    span_in = cols_tile if plan.forward else rows_tile
    plan = plan._replace(begun=bool(begun))
    out_shape = []
    scratch = [pltpu.VMEM((width, span_in), jnp.bfloat16)]
    for out in plan.outs:
        many = len(out.ks)
        if out.stacked:
            out_shape += [jax.ShapeDtypeStruct((many, width, wide), out.kind)]
        else:
            out_shape += [jax.ShapeDtypeStruct((1, width, wide), out.kind)] * many
        if not out.direct:
            scratch += [pltpu.VMEM((many, width, wide), jnp.float32)]
    if plan.fetched:
        scratch += [pltpu.VMEM(tiles.shape, tiles.dtype), pltpu.SemaphoreType.DMA((slots,))]
    vmem = pl.BlockSpec(memory_space=pltpu.VMEM)
    flat = pl.pallas_call(
        functools.partial(sweep_kernel, plan, parts[0].shape[2] // span_in),
        out_shape=out_shape,
        in_specs=[
            pl.BlockSpec(memory_space=pltpu.SMEM),
            pl.BlockSpec(memory_space=pl.ANY) if plan.fetched else vmem,
        ]
        + [vmem] * (len(parts) + len(begun)),
        out_specs=[vmem] * len(out_shape),
        scratch_shapes=scratch,
        compiler_params=pltpu.CompilerParams(
            vmem_limit_bytes=FETCH_LIMIT if plan.fetched else VMEM_LIMIT
        ),
        cost_estimate=pl.CostEstimate(
            flops=slots * width * rows_tile * cols_tile,
            bytes_accessed=tiles.size,
            transcendentals=0,
        ),
        name="forward_sweep" if plan.forward else "transpose_sweep",
    )(info, tiles, *parts, *begun)
    flat = list(flat)
    return [
        flat.pop(0) if out.stacked else {k: flat.pop(0) for k in out.ks} for out in plan.outs
    ]


def swap(value, axis, size, k):
    return lax.ppermute(value, axis, [(i, i ^ k) for i in range(size)])


def gather_pairs(own, axis, size):
    parts = [None] * size
    parts[0] = own
    for k in range(size - 2, 0, -2):
        parts[k] = swap(own, axis, size, k)
    for k in range(size - 2, -1, -2):
        parts[k + 1] = swap(parts[k], axis, size, 1)
    return parts


def update_kernel(shares, last, *refs):
    parts, (own, demand, kind, dual), outs = refs[:shares], refs[shares : shares + 4], refs[shares + 4 :]
    push = own[0]
    for part in parts:
        push = push + part[0].astype(jnp.float32)
    moved = dual[...] + step_dual * (demand[...] - push)
    moved = jnp.where(kind[...] == 1, jnp.maximum(moved, 0.0), moved)
    if last:
        outs[0][:, 0, :] = moved
    else:
        outs[0][...] = moved
        outs[1][0] = moved.astype(outs[1].dtype)


def update_dual(parts, own, demand, kind, dual, last):
    width, span = dual.shape
    vmem = pl.BlockSpec(memory_space=pltpu.VMEM)
    if last:
        out_shape = [jax.ShapeDtypeStruct((width, 1, span), jnp.float32)]
    else:
        out_shape = [
            jax.ShapeDtypeStruct((width, span), jnp.float32),
            jax.ShapeDtypeStruct((1, width, span), jnp.bfloat16),
        ]
    return pl.pallas_call(
        functools.partial(update_kernel, len(parts), last),
        out_shape=out_shape,
        in_specs=[vmem] * (len(parts) + 4),
        out_specs=[vmem] * len(out_shape),
        compiler_params=pltpu.CompilerParams(vmem_limit_bytes=VMEM_LIMIT),
        cost_estimate=pl.CostEstimate(
            flops=width * span * 16, bytes_accessed=width * span * 16, transcendentals=0
        ),
        name="update_dual",
    )(*parts, own, demand, kind, dual)


def share_pairs(kept, sent, axis, size):
    shares = {}
    for k in range(4, size, 2):
        pair = kept[k] + swap(sent[k + 1], axis, size, 1).astype(jnp.float32)
        shares[k] = swap(pair.astype(jnp.bfloat16), axis, size, k)
    for k in range(1, min(size, 4)):
        shares[k] = swap(sent[k], axis, size, k)
    return list(shares.values())


def sum_halves(kept, sent, axis, size):
    here = kept + swap(sent, axis, size, 1).astype(jnp.float32)
    away = here.astype(jnp.bfloat16)
    total = here
    for t in range(1, size // 2):
        other = swap(away, axis, size, 2 * t)
        order = [h ^ t for h in range(size // 2)]
        total = total + jnp.stack([other[h] for h in order]).astype(jnp.float32)
    return total


def body(
    rows,
    cols,
    tiles,
    tile_index,
    tile_count,
    weights,
    carbon,
    completion,
    demand,
    row_kind,
    primal_start,
    dual_start,
):
    blocks = tiles[0, 0]
    info = jnp.concatenate(
        [
            tile_index.reshape(-1),
            tile_count.reshape(-1),
            lax.axis_index("col")[None],
            lax.axis_index("row")[None],
        ]
    ).astype(jnp.int32)
    info_back = jnp.concatenate([info[:-2], info[-1:], info[-2:-1]])
    dual = dual_start[:, 0, :]
    rounded_dual = [dual.astype(jnp.bfloat16)[None]]
    state = jnp.concatenate([primal_start[:, 0, :], carbon, completion])
    states = [state] + [swap(state, "row", rows, k) for k in range(2, rows, 2)]
    states = jnp.stack(states)
    width = weights.shape[0]
    primal = states[:, :width]
    share = weights[:, None]
    cost = share * states[:, width : width + 1] + (1.0 - share) * states[:, width + 1 :]
    whole, rounded = jnp.float32, jnp.bfloat16
    late = [k for k in range(5, cols, 2)]
    early = [k for k in range(cols) if k not in late]
    mine, other = (tuple(range(p, rows, 2)) for p in (0, 1))
    keep = tuple(k for k in range(cols) if k % 2 == 0 and k != 2)
    send = tuple(k for k in range(cols) if k not in keep)
    for step in range(ITERS):
        dual_parts = gather_pairs(rounded_dual[0], "col", cols)
        begun = sweep(
            Plan(
                False, step == 0, tuple((k,) for k in early),
                (Out(mine, whole, True), Out(other, whole, True)), False,
            ),
            blocks, info, [dual_parts[k] for k in early], [], primal.shape[2],
        )
        kept, sent = sweep(
            Plan(
                False, False, tuple((k,) for k in late),
                (Out(mine, whole, True), Out(other, rounded, True)), True,
            ),
            blocks, info, [dual_parts[k] for k in late], begun, primal.shape[2],
        )
        pull = sum_halves(kept, sent, "row", rows)
        fresh = jnp.maximum(primal - step_primal * (cost - pull), 0.0)
        extra = (2.0 * fresh - primal).astype(jnp.bfloat16)
        primal = fresh
        kept, sent = sweep(
            Plan(
                True, False, (mine,),
                (Out(keep, whole, True), Out(send, whole, True)), False,
            ),
            blocks, info_back, [extra], [], dual.shape[1],
        )
        extra = swap(extra, "row", rows, 1)
        (sent,) = sweep(
            Plan(True, False, (other,), (Out(send, rounded, False),), True),
            blocks, info_back, [extra], [sent], dual.shape[1],
        )
        (kept,) = sweep(
            Plan(True, False, (other,), (Out(keep, whole, False),), True),
            blocks, info_back, [extra], [kept], dual.shape[1],
        )
        shares = share_pairs(kept, sent, "col", cols)
        dual, *rounded_dual = update_dual(
            shares, kept[0], demand, row_kind, dual, step == ITERS - 1
        )
    return (primal[0][:, None, :], dual)


def solution(mesh):
    placed = (
        P("row", "col", None, None, None),
        P("row", "col", None, None),
        P("row", "col"),
        P(),
        P("col", "row"),
        P("col", "row"),
        P("row", "col"),
        P("row", "col"),
        P(None, "col", "row"),
        P(None, "row", "col"),
    )
    return jax.shard_map(
        functools.partial(body, mesh.shape["row"], mesh.shape["col"]),
        mesh=mesh,
        in_specs=placed,
        out_specs=(P(None, "col", "row"), P(None, "row", "col")),
        check_vma=False,
    )
```

```python
import functools
import typing

import jax
import jax.numpy as jnp
from jax import lax
from jax.experimental import pallas as pl
from jax.experimental.pallas import tpu as pltpu
from jax.sharding import PartitionSpec as P

BR_DEV = 16
BC_DEV = 16
ITERS = 2


step_primal = 0.4
step_dual = 0.4

VMEM_LIMIT = 24 * 1024 * 1024
FETCH_LIMIT = 46 * 1024 * 1024


def among(value, ks):
    return functools.reduce(jnp.logical_or, [value == k for k in ks])


def position(value, ks):
    at = 0
    for i, k in enumerate(ks[1:]):
        at = jnp.where(value == k, i + 1, at)
    return at


class Out(typing.NamedTuple):
    ks: tuple
    kind: typing.Any
    stacked: bool

    @property
    def direct(self):
        return self.kind == jnp.float32 and self.stacked


class Plan(typing.NamedTuple):
    forward: bool
    fetched: bool
    senders: tuple
    outs: tuple
    begun: bool


def sweep_kernel(plan, per_in, info, tiles, *refs):
    refs = list(refs)
    parts = [refs.pop(0) for _ in plan.senders]
    begun = [refs.pop(0) for _ in plan.outs] if plan.begun else []
    results = [[refs.pop(0) for _ in (out.ks[:1] if out.stacked else out.ks)] for out in plan.outs]
    operand = refs.pop(0)
    sums = [
        result[0] if out.direct else refs.pop(0) for out, result in zip(plan.outs, results)
    ]
    held, arrived = refs if plan.fetched else (tiles, None)
    slots = tiles.shape[0]
    live = info[2 * slots]
    me_in = info[2 * slots + 1]
    me_out = info[2 * slots + 2]
    span_in = operand.shape[1]
    span_out = tiles.shape[1] if plan.forward else tiles.shape[2]
    per_out = sums[0].shape[2] // span_out

    def ends(slot):
        row, col = info[2 * slot], info[2 * slot + 1]
        return (col, row) if plan.forward else (row, col)

    def accepted(slot):
        block_in, block_out = ends(slot)
        source = (block_in // per_in) ^ me_in
        target = (block_out // per_out) ^ me_out
        return among(source, sum(plan.senders, ())) & among(
            target, sum((out.ks for out in plan.outs), ())
        )

    def fetch(slot):
        return pltpu.make_async_copy(tiles.at[slot], held.at[slot], arrived.at[slot])

    if plan.fetched:

        def start(slot, carry):
            @pl.when(accepted(slot))
            def _():
                fetch(slot).start()

            return carry

        lax.fori_loop(0, live, start, 0)
    for i, total in enumerate(sums):
        total[...] = begun[i][...] if begun else jnp.zeros_like(total)

    def visit(slot, carry):
        @pl.when(accepted(slot))
        def _():
            block_in, block_out = ends(slot)
            source = (block_in // per_in) ^ me_in
            target = (block_out // per_out) ^ me_out
            place = pl.multiple_of((block_in % per_in) * span_in, span_in)
            for part, ks in zip(parts, plan.senders):

                @pl.when(among(source, ks))
                def _():
                    operand[...] = part[position(source, ks), :, pl.ds(place, span_in)]

            if plan.fetched:
                fetch(slot).wait()
            contract = (((1,), (1,)), ((), ())) if plan.forward else (((1,), (0,)), ((), ()))
            term = lax.dot_general(
                operand[...], held[slot], contract, preferred_element_type=jnp.float32
            )
            to = pl.multiple_of((block_out % per_out) * span_out, span_out)
            for total, out in zip(sums, plan.outs):

                @pl.when(among(target, out.ks))
                def _():
                    total[position(target, out.ks), :, pl.ds(to, span_out)] += term

        return carry

    lax.fori_loop(0, live, visit, 0)
    for out, result, total in zip(plan.outs, results, sums):
        if not out.direct:
            each = len(out.ks) // len(result)
            for i, ref in enumerate(result):
                ref[...] = total[i * each : (i + 1) * each].astype(ref.dtype)


def sweep(plan, tiles, info, parts, begun, wide):
    slots, rows_tile, cols_tile = tiles.shape
    width = parts[0].shape[1]
    span_in = cols_tile if plan.forward else rows_tile
    plan = plan._replace(begun=bool(begun))
    out_shape = []
    scratch = [pltpu.VMEM((width, span_in), jnp.bfloat16)]
    for out in plan.outs:
        many = len(out.ks)
        if out.stacked:
            out_shape += [jax.ShapeDtypeStruct((many, width, wide), out.kind)]
        else:
            out_shape += [jax.ShapeDtypeStruct((1, width, wide), out.kind)] * many
        if not out.direct:
            scratch += [pltpu.VMEM((many, width, wide), jnp.float32)]
    if plan.fetched:
        scratch += [pltpu.VMEM(tiles.shape, tiles.dtype), pltpu.SemaphoreType.DMA((slots,))]
    vmem = pl.BlockSpec(memory_space=pltpu.VMEM)
    flat = pl.pallas_call(
        functools.partial(sweep_kernel, plan, parts[0].shape[2] // span_in),
        out_shape=out_shape,
        in_specs=[
            pl.BlockSpec(memory_space=pltpu.SMEM),
            pl.BlockSpec(memory_space=pl.ANY) if plan.fetched else vmem,
        ]
        + [vmem] * (len(parts) + len(begun)),
        out_specs=[vmem] * len(out_shape),
        scratch_shapes=scratch,
        compiler_params=pltpu.CompilerParams(
            vmem_limit_bytes=FETCH_LIMIT if plan.fetched else VMEM_LIMIT
        ),
        cost_estimate=pl.CostEstimate(
            flops=slots * width * rows_tile * cols_tile,
            bytes_accessed=tiles.size,
            transcendentals=0,
        ),
        name="forward_sweep" if plan.forward else "transpose_sweep",
    )(info, tiles, *parts, *begun)
    flat = list(flat)
    return [
        flat.pop(0) if out.stacked else {k: flat.pop(0) for k in out.ks} for out in plan.outs
    ]


def swap(value, axis, size, k):
    return lax.ppermute(value, axis, [(i, i ^ k) for i in range(size)])


def strides(size):
    return sorted(range(2, size, 2), key=lambda k: (k % 4 == 0, -k))


def gather_pairs(own, axis, size):
    parts = [None] * size
    parts[0] = own
    for k in strides(size):
        parts[k] = swap(own, axis, size, k)
    for k in [0] + strides(size):
        parts[k + 1] = swap(parts[k], axis, size, 1)
    return parts


def update_kernel(shares, last, *refs):
    parts, (own, demand, kind, dual), outs = refs[:shares], refs[shares : shares + 4], refs[shares + 4 :]
    push = own[0]
    for part in parts:
        push = push + part[0].astype(jnp.float32)
    moved = dual[...] + step_dual * (demand[...] - push)
    moved = jnp.where(kind[...] == 1, jnp.maximum(moved, 0.0), moved)
    if last:
        outs[0][:, 0, :] = moved
    else:
        outs[0][...] = moved
        outs[1][0] = moved.astype(outs[1].dtype)


def update_dual(parts, own, demand, kind, dual, last):
    width, span = dual.shape
    vmem = pl.BlockSpec(memory_space=pltpu.VMEM)
    if last:
        out_shape = [jax.ShapeDtypeStruct((width, 1, span), jnp.float32)]
    else:
        out_shape = [
            jax.ShapeDtypeStruct((width, span), jnp.float32),
            jax.ShapeDtypeStruct((1, width, span), jnp.bfloat16),
        ]
    return pl.pallas_call(
        functools.partial(update_kernel, len(parts), last),
        out_shape=out_shape,
        in_specs=[vmem] * (len(parts) + 4),
        out_specs=[vmem] * len(out_shape),
        compiler_params=pltpu.CompilerParams(vmem_limit_bytes=VMEM_LIMIT),
        cost_estimate=pl.CostEstimate(
            flops=width * span * 16, bytes_accessed=width * span * 16, transcendentals=0
        ),
        name="update_dual",
    )(*parts, own, demand, kind, dual)


def share_pairs(kept, sent, axis, size):
    shares = []
    for k in strides(size)[::-1]:
        pair = kept[k] + swap(sent[k + 1], axis, size, 1).astype(jnp.float32)
        shares.append(swap(pair.astype(jnp.bfloat16), axis, size, k))
    return shares + [swap(sent[1], axis, size, 1)]


def sum_halves(kept, sent, axis, size):
    here = kept + swap(sent, axis, size, 1).astype(jnp.float32)
    away = here.astype(jnp.bfloat16)
    total = here
    for t in range(1, size // 2):
        other = swap(away, axis, size, 2 * t)
        order = [h ^ t for h in range(size // 2)]
        total = total + jnp.stack([other[h] for h in order]).astype(jnp.float32)
    return total


def body(
    rows,
    cols,
    tiles,
    tile_index,
    tile_count,
    weights,
    carbon,
    completion,
    demand,
    row_kind,
    primal_start,
    dual_start,
):
    blocks = tiles[0, 0]
    info = jnp.concatenate(
        [
            tile_index.reshape(-1),
            tile_count.reshape(-1),
            lax.axis_index("col")[None],
            lax.axis_index("row")[None],
        ]
    ).astype(jnp.int32)
    info_back = jnp.concatenate([info[:-2], info[-1:], info[-2:-1]])
    dual = dual_start[:, 0, :]
    rounded_dual = [dual.astype(jnp.bfloat16)[None]]
    state = jnp.concatenate([primal_start[:, 0, :], carbon, completion])
    states = [state] + [swap(state, "row", rows, k) for k in range(2, rows, 2)]
    states = jnp.stack(states)
    width = weights.shape[0]
    primal = states[:, :width]
    share = weights[:, None]
    cost = share * states[:, width : width + 1] + (1.0 - share) * states[:, width + 1 :]
    whole, rounded = jnp.float32, jnp.bfloat16
    order = [k for pair in strides(cols)[::-1] + [0] for k in (pair + 1, pair)]
    mine, other = (tuple(range(p, rows, 2)) for p in (0, 1))
    keep, send = (tuple(range(p, cols, 2)) for p in (0, 1))
    for step in range(ITERS):
        dual_parts = gather_pairs(rounded_dual[0], "col", cols)
        sent, kept = [
            sweep(
                Plan(
                    False, step == 0, tuple((k,) for k in order),
                    (Out(other, rounded, True) if sending else Out(mine, whole, True),), False,
                ),
                blocks, info, [dual_parts[k] for k in order], [], primal.shape[2],
            )[0]
            for sending in (True, False)
        ]
        pull = sum_halves(kept, sent, "row", rows)
        fresh = jnp.maximum(primal - step_primal * (cost - pull), 0.0)
        extra = (2.0 * fresh - primal).astype(jnp.bfloat16)
        primal = fresh
        extra = [extra, swap(extra, "row", rows, 1)]
        (sent,) = sweep(
            Plan(True, False, (mine, other), (Out(send, rounded, False),), False),
            blocks, info_back, extra, [], dual.shape[1],
        )
        (kept,) = sweep(
            Plan(True, False, (mine, other), (Out(keep, whole, False),), False),
            blocks, info_back, extra, [], dual.shape[1],
        )
        shares = share_pairs(kept, sent, "col", cols)
        dual, *rounded_dual = update_dual(
            shares, kept[0], demand, row_kind, dual, step == ITERS - 1
        )
    return (primal[0][:, None, :], dual)


def solution(mesh):
    placed = (
        P("row", "col", None, None, None),
        P("row", "col", None, None),
        P("row", "col"),
        P(),
        P("col", "row"),
        P("col", "row"),
        P("row", "col"),
        P("row", "col"),
        P(None, "col", "row"),
        P(None, "row", "col"),
    )
    return jax.shard_map(
        functools.partial(body, mesh.shape["row"], mesh.shape["col"]),
        mesh=mesh,
        in_specs=placed,
        out_specs=(P(None, "col", "row"), P(None, "row", "col")),
        check_vma=False,
    )
```

```python
import functools
import typing

import jax
import jax.numpy as jnp
from jax import lax
from jax.experimental import pallas as pl
from jax.experimental.pallas import tpu as pltpu
from jax.sharding import PartitionSpec as P

BR_DEV = 16
BC_DEV = 16
ITERS = 2


step_primal = 0.4
step_dual = 0.4

VMEM_LIMIT = 24 * 1024 * 1024
FETCH_LIMIT = 46 * 1024 * 1024


def among(value, ks):
    return functools.reduce(jnp.logical_or, [value == k for k in ks])


def position(value, ks):
    at = 0
    for i, k in enumerate(ks[1:]):
        at = jnp.where(value == k, i + 1, at)
    return at


class Out(typing.NamedTuple):
    ks: tuple
    kind: typing.Any
    stacked: bool

    @property
    def direct(self):
        return self.kind == jnp.float32 and self.stacked


class Plan(typing.NamedTuple):
    forward: bool
    fetched: bool
    senders: tuple
    outs: tuple
    begun: bool


def sweep_kernel(plan, per_in, info, tiles, *refs):
    refs = list(refs)
    parts = [refs.pop(0) for _ in plan.senders]
    begun = [refs.pop(0) for _ in plan.outs] if plan.begun else []
    results = [[refs.pop(0) for _ in (out.ks[:1] if out.stacked else out.ks)] for out in plan.outs]
    operand = refs.pop(0)
    sums = [
        result[0] if out.direct else refs.pop(0) for out, result in zip(plan.outs, results)
    ]
    held, arrived = refs if plan.fetched else (tiles, None)
    slots = tiles.shape[0]
    live = info[2 * slots]
    me_in = info[2 * slots + 1]
    me_out = info[2 * slots + 2]
    span_in = operand.shape[1]
    span_out = tiles.shape[1] if plan.forward else tiles.shape[2]
    per_out = sums[0].shape[2] // span_out

    def ends(slot):
        row, col = info[2 * slot], info[2 * slot + 1]
        return (col, row) if plan.forward else (row, col)

    def accepted(slot):
        block_in, block_out = ends(slot)
        source = (block_in // per_in) ^ me_in
        target = (block_out // per_out) ^ me_out
        return among(source, sum(plan.senders, ())) & among(
            target, sum((out.ks for out in plan.outs), ())
        )

    def fetch(slot):
        return pltpu.make_async_copy(tiles.at[slot], held.at[slot], arrived.at[slot])

    if plan.fetched:

        def start(slot, carry):
            @pl.when(accepted(slot))
            def _():
                fetch(slot).start()

            return carry

        lax.fori_loop(0, live, start, 0)
    for i, total in enumerate(sums):
        total[...] = begun[i][...] if begun else jnp.zeros_like(total)

    def visit(slot, carry):
        @pl.when(accepted(slot))
        def _():
            block_in, block_out = ends(slot)
            source = (block_in // per_in) ^ me_in
            target = (block_out // per_out) ^ me_out
            place = pl.multiple_of((block_in % per_in) * span_in, span_in)
            for part, ks in zip(parts, plan.senders):

                @pl.when(among(source, ks))
                def _():
                    operand[...] = part[position(source, ks), :, pl.ds(place, span_in)]

            if plan.fetched:
                fetch(slot).wait()
            contract = (((1,), (1,)), ((), ())) if plan.forward else (((1,), (0,)), ((), ()))
            term = lax.dot_general(
                operand[...], held[slot], contract, preferred_element_type=jnp.float32
            )
            to = pl.multiple_of((block_out % per_out) * span_out, span_out)
            for total, out in zip(sums, plan.outs):

                @pl.when(among(target, out.ks))
                def _():
                    total[position(target, out.ks), :, pl.ds(to, span_out)] += term

        return carry

    lax.fori_loop(0, live, visit, 0)
    for out, result, total in zip(plan.outs, results, sums):
        if not out.direct:
            each = len(out.ks) // len(result)
            for i, ref in enumerate(result):
                ref[...] = total[i * each : (i + 1) * each].astype(ref.dtype)


def sweep(plan, tiles, info, parts, begun, wide):
    slots, rows_tile, cols_tile = tiles.shape
    width = parts[0].shape[1]
    span_in = cols_tile if plan.forward else rows_tile
    plan = plan._replace(begun=bool(begun))
    out_shape = []
    scratch = [pltpu.VMEM((width, span_in), jnp.bfloat16)]
    for out in plan.outs:
        many = len(out.ks)
        if out.stacked:
            out_shape += [jax.ShapeDtypeStruct((many, width, wide), out.kind)]
        else:
            out_shape += [jax.ShapeDtypeStruct((1, width, wide), out.kind)] * many
        if not out.direct:
            scratch += [pltpu.VMEM((many, width, wide), jnp.float32)]
    if plan.fetched:
        scratch += [pltpu.VMEM(tiles.shape, tiles.dtype), pltpu.SemaphoreType.DMA((slots,))]
    vmem = pl.BlockSpec(memory_space=pltpu.VMEM)
    flat = pl.pallas_call(
        functools.partial(sweep_kernel, plan, parts[0].shape[2] // span_in),
        out_shape=out_shape,
        in_specs=[
            pl.BlockSpec(memory_space=pltpu.SMEM),
            pl.BlockSpec(memory_space=pl.ANY) if plan.fetched else vmem,
        ]
        + [vmem] * (len(parts) + len(begun)),
        out_specs=[vmem] * len(out_shape),
        scratch_shapes=scratch,
        compiler_params=pltpu.CompilerParams(
            vmem_limit_bytes=FETCH_LIMIT if plan.fetched else VMEM_LIMIT
        ),
        cost_estimate=pl.CostEstimate(
            flops=slots * width * rows_tile * cols_tile,
            bytes_accessed=tiles.size,
            transcendentals=0,
        ),
        name="forward_sweep" if plan.forward else "transpose_sweep",
    )(info, tiles, *parts, *begun)
    flat = list(flat)
    return [
        flat.pop(0) if out.stacked else {k: flat.pop(0) for k in out.ks} for out in plan.outs
    ]


def swap(value, axis, size, k):
    return lax.ppermute(value, axis, [(i, i ^ k) for i in range(size)])


def strides(size):
    return sorted(range(2, size, 2), key=lambda k: (k % 4 == 0, -k))


def gather_pairs(own, axis, size):
    parts = [None] * size
    parts[0] = own
    for k in strides(size):
        parts[k] = swap(own, axis, size, k)
    for k in [0] + strides(size):
        parts[k + 1] = swap(parts[k], axis, size, 1)
    return parts


def update_kernel(shares, last, *refs):
    parts, (own, demand, kind, dual), outs = refs[:shares], refs[shares : shares + 4], refs[shares + 4 :]
    push = own[0]
    for part in parts:
        push = push + part[0].astype(jnp.float32)
    moved = dual[...] + step_dual * (demand[...] - push)
    moved = jnp.where(kind[...] == 1, jnp.maximum(moved, 0.0), moved)
    if last:
        outs[0][:, 0, :] = moved
    else:
        outs[0][...] = moved
        outs[1][0] = moved.astype(outs[1].dtype)


def update_dual(parts, own, demand, kind, dual, last):
    width, span = dual.shape
    vmem = pl.BlockSpec(memory_space=pltpu.VMEM)
    if last:
        out_shape = [jax.ShapeDtypeStruct((width, 1, span), jnp.float32)]
    else:
        out_shape = [
            jax.ShapeDtypeStruct((width, span), jnp.float32),
            jax.ShapeDtypeStruct((1, width, span), jnp.bfloat16),
        ]
    return pl.pallas_call(
        functools.partial(update_kernel, len(parts), last),
        out_shape=out_shape,
        in_specs=[vmem] * (len(parts) + 4),
        out_specs=[vmem] * len(out_shape),
        compiler_params=pltpu.CompilerParams(vmem_limit_bytes=VMEM_LIMIT),
        cost_estimate=pl.CostEstimate(
            flops=width * span * 16, bytes_accessed=width * span * 16, transcendentals=0
        ),
        name="update_dual",
    )(*parts, own, demand, kind, dual)


def share_pairs(kept, sent, axis, size):
    shares = []
    for k in strides(size)[::-1]:
        pair = kept[k] + swap(sent[k + 1], axis, size, 1).astype(jnp.float32)
        shares.append(swap(pair.astype(jnp.bfloat16), axis, size, k))
    return shares + [swap(sent[1], axis, size, 1)]


def sum_halves(kept, sent, axis, size):
    here = kept + swap(sent, axis, size, 1).astype(jnp.float32)
    away = here.astype(jnp.bfloat16)
    total = here
    for t in range(1, size // 2):
        other = swap(away, axis, size, 2 * t)
        order = [h ^ t for h in range(size // 2)]
        total = total + jnp.stack([other[h] for h in order]).astype(jnp.float32)
    return total


def body(
    rows,
    cols,
    tiles,
    tile_index,
    tile_count,
    weights,
    carbon,
    completion,
    demand,
    row_kind,
    primal_start,
    dual_start,
):
    blocks = tiles[0, 0]
    info = jnp.concatenate(
        [
            tile_index.reshape(-1),
            tile_count.reshape(-1),
            lax.axis_index("col")[None],
            lax.axis_index("row")[None],
        ]
    ).astype(jnp.int32)
    info_back = jnp.concatenate([info[:-2], info[-1:], info[-2:-1]])
    dual = dual_start[:, 0, :]
    rounded_dual = [dual.astype(jnp.bfloat16)[None]]
    state = jnp.concatenate([primal_start[:, 0, :], carbon, completion])
    states = [state] + [swap(state, "row", rows, k) for k in range(2, rows, 2)]
    states = jnp.stack(states)
    width = weights.shape[0]
    primal = states[:, :width]
    share = weights[:, None]
    cost = share * states[:, width : width + 1] + (1.0 - share) * states[:, width + 1 :]
    whole, rounded = jnp.float32, jnp.bfloat16
    order = [k for pair in strides(cols)[::-1] + [0] for k in (pair + 1, pair)]
    mine, other = (tuple(range(p, rows, 2)) for p in (0, 1))
    keep = tuple(range(0, cols, 2))
    leave = [k + 1 for k in strides(cols)[::-1] + [0]]
    first, then = tuple(leave[:2]), tuple(leave[2:])
    for step in range(ITERS):
        dual_parts = gather_pairs(rounded_dual[0], "col", cols)
        sent, kept = [
            sweep(
                Plan(
                    False, step == 0, tuple((k,) for k in order),
                    (Out(other, rounded, True) if sending else Out(mine, whole, True),), False,
                ),
                blocks, info, [dual_parts[k] for k in order], [], primal.shape[2],
            )[0]
            for sending in (True, False)
        ]
        pull = sum_halves(kept, sent, "row", rows)
        fresh = jnp.maximum(primal - step_primal * (cost - pull), 0.0)
        extra = (2.0 * fresh - primal).astype(jnp.bfloat16)
        primal = fresh
        extra = [extra, swap(extra, "row", rows, 1)]
        (sent,) = sweep(
            Plan(True, False, (mine, other), (Out(first, rounded, False),), False),
            blocks, info_back, extra, [], dual.shape[1],
        )
        rest, kept = sweep(
            Plan(
                True, False, (mine, other),
                (Out(then, rounded, False), Out(keep, whole, False)), False,
            ),
            blocks, info_back, extra, [], dual.shape[1],
        )
        sent |= rest
        shares = share_pairs(kept, sent, "col", cols)
        dual, *rounded_dual = update_dual(
            shares, kept[0], demand, row_kind, dual, step == ITERS - 1
        )
    return (primal[0][:, None, :], dual)


def solution(mesh):
    placed = (
        P("row", "col", None, None, None),
        P("row", "col", None, None),
        P("row", "col"),
        P(),
        P("col", "row"),
        P("col", "row"),
        P("row", "col"),
        P("row", "col"),
        P(None, "col", "row"),
        P(None, "row", "col"),
    )
    return jax.shard_map(
        functools.partial(body, mesh.shape["row"], mesh.shape["col"]),
        mesh=mesh,
        in_specs=placed,
        out_specs=(P(None, "col", "row"), P(None, "row", "col")),
        check_vma=False,
    )
```

```python
import functools
import typing

import jax
import jax.numpy as jnp
from jax import lax
from jax.experimental import pallas as pl
from jax.experimental.pallas import tpu as pltpu
from jax.sharding import PartitionSpec as P

BR_DEV = 16
BC_DEV = 16
ITERS = 2


step_primal = 0.4
step_dual = 0.4

VMEM_LIMIT = 24 * 1024 * 1024
FETCH_LIMIT = 46 * 1024 * 1024
LOAD_LIMIT = 42 * 1024 * 1024


def among(value, ks):
    return functools.reduce(jnp.logical_or, [value == k for k in ks])


def position(value, ks):
    at = 0
    for i, k in enumerate(ks[1:]):
        at = jnp.where(value == k, i + 1, at)
    return at


class Out(typing.NamedTuple):
    ks: tuple
    kind: typing.Any
    stacked: bool

    @property
    def direct(self):
        return self.kind == jnp.float32 and self.stacked


class Plan(typing.NamedTuple):
    forward: bool
    fetched: bool
    senders: tuple
    outs: tuple
    begun: bool


def sweep_kernel(plan, per_in, info, tiles, *refs):
    refs = list(refs)
    parts = [refs.pop(0) for _ in plan.senders]
    begun = [refs.pop(0) for _ in plan.outs] if plan.begun else []
    results = [[refs.pop(0) for _ in (out.ks[:1] if out.stacked else out.ks)] for out in plan.outs]
    operand = refs.pop(0)
    sums = [
        result[0] if out.direct else refs.pop(0) for out, result in zip(plan.outs, results)
    ]
    held, arrived = refs if plan.fetched else (tiles, None)
    slots = tiles.shape[0]
    live = info[2 * slots]
    me_in = info[2 * slots + 1]
    me_out = info[2 * slots + 2]
    span_in = operand.shape[1]
    span_out = tiles.shape[1] if plan.forward else tiles.shape[2]
    per_out = sums[0].shape[2] // span_out

    def ends(slot):
        row, col = info[2 * slot], info[2 * slot + 1]
        return (col, row) if plan.forward else (row, col)

    def accepted(slot):
        block_in, block_out = ends(slot)
        source = (block_in // per_in) ^ me_in
        target = (block_out // per_out) ^ me_out
        return among(source, sum(plan.senders, ())) & among(
            target, sum((out.ks for out in plan.outs), ())
        )

    def fetch(slot):
        return pltpu.make_async_copy(tiles.at[slot], held.at[slot], arrived.at[slot])

    if plan.fetched:

        def start(slot, carry):
            @pl.when(accepted(slot))
            def _():
                fetch(slot).start()

            return carry

        lax.fori_loop(0, live, start, 0)
    for i, total in enumerate(sums):
        total[...] = begun[i][...] if begun else jnp.zeros_like(total)

    def visit(slot, carry):
        @pl.when(accepted(slot))
        def _():
            block_in, block_out = ends(slot)
            source = (block_in // per_in) ^ me_in
            target = (block_out // per_out) ^ me_out
            place = pl.multiple_of((block_in % per_in) * span_in, span_in)
            for part, ks in zip(parts, plan.senders):

                @pl.when(among(source, ks))
                def _():
                    operand[...] = part[position(source, ks), :, pl.ds(place, span_in)]

            if plan.fetched:
                fetch(slot).wait()
            contract = (((1,), (1,)), ((), ())) if plan.forward else (((1,), (0,)), ((), ()))
            term = lax.dot_general(
                operand[...], held[slot], contract, preferred_element_type=jnp.float32
            )
            to = pl.multiple_of((block_out % per_out) * span_out, span_out)
            for total, out in zip(sums, plan.outs):

                @pl.when(among(target, out.ks))
                def _():
                    total[position(target, out.ks), :, pl.ds(to, span_out)] += term

        return carry

    lax.fori_loop(0, live, visit, 0)
    for out, result, total in zip(plan.outs, results, sums):
        if not out.direct:
            each = len(out.ks) // len(result)
            for i, ref in enumerate(result):
                ref[...] = total[i * each : (i + 1) * each].astype(ref.dtype)


def sweep(plan, tiles, info, parts, begun, wide):
    slots, rows_tile, cols_tile = tiles.shape
    width = parts[0].shape[1]
    span_in = cols_tile if plan.forward else rows_tile
    plan = plan._replace(begun=bool(begun))
    out_shape = []
    scratch = [pltpu.VMEM((width, span_in), jnp.bfloat16)]
    for out in plan.outs:
        many = len(out.ks)
        if out.stacked:
            out_shape += [jax.ShapeDtypeStruct((many, width, wide), out.kind)]
        else:
            out_shape += [jax.ShapeDtypeStruct((1, width, wide), out.kind)] * many
        if not out.direct:
            scratch += [pltpu.VMEM((many, width, wide), jnp.float32)]
    if plan.fetched:
        scratch += [pltpu.VMEM(tiles.shape, tiles.dtype), pltpu.SemaphoreType.DMA((slots,))]
    vmem = pl.BlockSpec(memory_space=pltpu.VMEM)
    flat = pl.pallas_call(
        functools.partial(sweep_kernel, plan, parts[0].shape[2] // span_in),
        out_shape=out_shape,
        in_specs=[
            pl.BlockSpec(memory_space=pltpu.SMEM),
            pl.BlockSpec(memory_space=pl.ANY) if plan.fetched else vmem,
        ]
        + [vmem] * (len(parts) + len(begun)),
        out_specs=[vmem] * len(out_shape),
        scratch_shapes=scratch,
        compiler_params=pltpu.CompilerParams(
            vmem_limit_bytes=FETCH_LIMIT if plan.fetched else VMEM_LIMIT
        ),
        cost_estimate=pl.CostEstimate(
            flops=slots * width * rows_tile * cols_tile,
            bytes_accessed=tiles.size,
            transcendentals=0,
        ),
        name="forward_sweep" if plan.forward else "transpose_sweep",
    )(info, tiles, *parts, *begun)
    flat = list(flat)
    return [
        flat.pop(0) if out.stacked else {k: flat.pop(0) for k in out.ks} for out in plan.outs
    ]


def load_kernel(info, tiles, held, arrived):
    live = info[2 * tiles.shape[0]]

    def fetch(slot):
        return pltpu.make_async_copy(tiles.at[slot], held.at[slot], arrived.at[slot])

    def start(slot, carry):
        fetch(slot).start()
        return carry

    def finish(slot, carry):
        fetch(slot).wait()
        return carry

    lax.fori_loop(0, live, start, 0)
    lax.fori_loop(0, live, finish, 0)


def load_tiles(info, tiles):
    return pl.pallas_call(
        load_kernel,
        out_shape=jax.ShapeDtypeStruct(tiles.shape, tiles.dtype),
        in_specs=[pl.BlockSpec(memory_space=pltpu.SMEM), pl.BlockSpec(memory_space=pl.ANY)],
        out_specs=pl.BlockSpec(memory_space=pltpu.VMEM),
        scratch_shapes=[pltpu.SemaphoreType.DMA((tiles.shape[0],))],
        compiler_params=pltpu.CompilerParams(vmem_limit_bytes=LOAD_LIMIT),
        cost_estimate=pl.CostEstimate(
            flops=0, bytes_accessed=4 * tiles.size, transcendentals=0
        ),
        name="load_tiles",
    )(info, tiles)


def swap(value, axis, size, k):
    return lax.ppermute(value, axis, [(i, i ^ k) for i in range(size)])


def strides(size):
    return sorted(range(2, size, 2), key=lambda k: (k % 4 == 0, -k))


def gather_pairs(own, axis, size):
    parts = [None] * size
    parts[0] = own
    for k in strides(size):
        parts[k] = swap(own, axis, size, k)
    for k in [0] + strides(size):
        parts[k + 1] = swap(parts[k], axis, size, 1)
    return parts


def update_kernel(shares, last, *refs):
    parts, (own, demand, kind, dual), outs = refs[:shares], refs[shares : shares + 4], refs[shares + 4 :]
    push = own[0]
    for part in parts:
        push = push + part[0].astype(jnp.float32)
    moved = dual[...] + step_dual * (demand[...] - push)
    moved = jnp.where(kind[...] == 1, jnp.maximum(moved, 0.0), moved)
    if last:
        outs[0][:, 0, :] = moved
    else:
        outs[0][...] = moved
        outs[1][0] = moved.astype(outs[1].dtype)


def update_dual(parts, own, demand, kind, dual, last):
    width, span = dual.shape
    vmem = pl.BlockSpec(memory_space=pltpu.VMEM)
    if last:
        out_shape = [jax.ShapeDtypeStruct((width, 1, span), jnp.float32)]
    else:
        out_shape = [
            jax.ShapeDtypeStruct((width, span), jnp.float32),
            jax.ShapeDtypeStruct((1, width, span), jnp.bfloat16),
        ]
    return pl.pallas_call(
        functools.partial(update_kernel, len(parts), last),
        out_shape=out_shape,
        in_specs=[vmem] * (len(parts) + 4),
        out_specs=[vmem] * len(out_shape),
        compiler_params=pltpu.CompilerParams(vmem_limit_bytes=VMEM_LIMIT),
        cost_estimate=pl.CostEstimate(
            flops=width * span * 16, bytes_accessed=width * span * 16, transcendentals=0
        ),
        name="update_dual",
    )(*parts, own, demand, kind, dual)


def share_pairs(kept, sent, axis, size):
    shares = []
    for k in strides(size)[::-1]:
        pair = kept[k] + swap(sent[k + 1], axis, size, 1).astype(jnp.float32)
        shares.append(swap(pair.astype(jnp.bfloat16), axis, size, k))
    return shares + [swap(sent[1], axis, size, 1)]


def sum_halves(kept, sent, axis, size):
    here = kept + swap(sent, axis, size, 1).astype(jnp.float32)
    away = here.astype(jnp.bfloat16)
    total = here
    for t in range(1, size // 2):
        other = swap(away, axis, size, 2 * t)
        order = [h ^ t for h in range(size // 2)]
        total = total + jnp.stack([other[h] for h in order]).astype(jnp.float32)
    return total


def body(
    rows,
    cols,
    tiles,
    tile_index,
    tile_count,
    weights,
    carbon,
    completion,
    demand,
    row_kind,
    primal_start,
    dual_start,
):
    blocks = tiles[0, 0]
    info = jnp.concatenate(
        [
            tile_index.reshape(-1),
            tile_count.reshape(-1),
            lax.axis_index("col")[None],
            lax.axis_index("row")[None],
        ]
    ).astype(jnp.int32)
    info_back = jnp.concatenate([info[:-2], info[-1:], info[-2:-1]])
    dual = dual_start[:, 0, :]
    rounded_dual = [dual.astype(jnp.bfloat16)[None]]
    state = jnp.concatenate([primal_start[:, 0, :], carbon, completion])
    states = [state] + [swap(state, "row", rows, k) for k in range(2, rows, 2)]
    states = jnp.stack(states)
    width = weights.shape[0]
    primal = states[:, :width]
    share = weights[:, None]
    cost = share * states[:, width : width + 1] + (1.0 - share) * states[:, width + 1 :]
    whole, rounded = jnp.float32, jnp.bfloat16
    order = [k for pair in strides(cols)[::-1] + [0] for k in (pair + 1, pair)]
    mine, other = (tuple(range(p, rows, 2)) for p in (0, 1))
    keep = tuple(range(0, cols, 2))
    leave = [k + 1 for k in strides(cols)[::-1] + [0]]
    first, then = tuple(leave[:2]), tuple(leave[2:])
    blocks = load_tiles(info, blocks)
    for step in range(ITERS):
        dual_parts = gather_pairs(rounded_dual[0], "col", cols)
        sent, kept = [
            sweep(
                Plan(
                    False, False, tuple((k,) for k in order),
                    (Out(other, rounded, True) if sending else Out(mine, whole, True),), False,
                ),
                blocks, info, [dual_parts[k] for k in order], [], primal.shape[2],
            )[0]
            for sending in (True, False)
        ]
        pull = sum_halves(kept, sent, "row", rows)
        fresh = jnp.maximum(primal - step_primal * (cost - pull), 0.0)
        extra = (2.0 * fresh - primal).astype(jnp.bfloat16)
        primal = fresh
        extra = [extra, swap(extra, "row", rows, 1)]
        (sent,) = sweep(
            Plan(True, False, (mine, other), (Out(first, rounded, False),), False),
            blocks, info_back, extra, [], dual.shape[1],
        )
        rest, kept = sweep(
            Plan(
                True, False, (mine, other),
                (Out(then, rounded, False), Out(keep, whole, False)), False,
            ),
            blocks, info_back, extra, [], dual.shape[1],
        )
        sent |= rest
        shares = share_pairs(kept, sent, "col", cols)
        dual, *rounded_dual = update_dual(
            shares, kept[0], demand, row_kind, dual, step == ITERS - 1
        )
    return (primal[0][:, None, :], dual)


def solution(mesh):
    placed = (
        P("row", "col", None, None, None),
        P("row", "col", None, None),
        P("row", "col"),
        P(),
        P("col", "row"),
        P("col", "row"),
        P("row", "col"),
        P("row", "col"),
        P(None, "col", "row"),
        P(None, "row", "col"),
    )
    return jax.shard_map(
        functools.partial(body, mesh.shape["row"], mesh.shape["col"]),
        mesh=mesh,
        in_specs=placed,
        out_specs=(P(None, "col", "row"), P(None, "row", "col")),
        check_vma=False,
    )
```

```python
import functools
import typing

import jax
import jax.numpy as jnp
from jax import lax
from jax.experimental import pallas as pl
from jax.experimental.pallas import tpu as pltpu
from jax.sharding import PartitionSpec as P

BR_DEV = 16
BC_DEV = 16
ITERS = 2


step_primal = 0.4
step_dual = 0.4

VMEM_LIMIT = 24 * 1024 * 1024
LOAD_LIMIT = 42 * 1024 * 1024


def among(value, ks):
    return functools.reduce(jnp.logical_or, [value == k for k in ks])


def position(value, ks):
    at = 0
    for i, k in enumerate(ks[1:]):
        at = jnp.where(value == k, i + 1, at)
    return at


class Out(typing.NamedTuple):
    ks: tuple
    kind: typing.Any
    stacked: bool

    @property
    def direct(self):
        return self.kind == jnp.float32 and self.stacked


class Plan(typing.NamedTuple):
    forward: bool
    senders: tuple
    outs: tuple
    begun: bool


def sweep_kernel(plan, per_in, places, live, tiles, *refs):
    refs = list(refs)
    parts = [refs.pop(0) for _ in plan.senders]
    begun = [refs.pop(0) for _ in plan.outs] if plan.begun else []
    results = [[refs.pop(0) for _ in (out.ks[:1] if out.stacked else out.ks)] for out in plan.outs]
    operand = refs.pop(0)
    sums = [
        result[0] if out.direct else refs.pop(0) for out, result in zip(plan.outs, results)
    ]
    me_in = lax.axis_index("row" if plan.forward else "col")
    me_out = lax.axis_index("col" if plan.forward else "row")
    span_in = operand.shape[1]
    span_out = tiles.shape[1] if plan.forward else tiles.shape[2]
    per_out = sums[0].shape[2] // span_out

    def ends(slot):
        row, col = places[0, slot], places[1, slot]
        return (col, row) if plan.forward else (row, col)

    def accepted(slot):
        block_in, block_out = ends(slot)
        source = (block_in // per_in) ^ me_in
        target = (block_out // per_out) ^ me_out
        return among(source, sum(plan.senders, ())) & among(
            target, sum((out.ks for out in plan.outs), ())
        )

    for i, total in enumerate(sums):
        total[...] = begun[i][...] if begun else jnp.zeros_like(total)

    def visit(slot, carry):
        @pl.when(accepted(slot))
        def _():
            block_in, block_out = ends(slot)
            source = (block_in // per_in) ^ me_in
            target = (block_out // per_out) ^ me_out
            place = pl.multiple_of((block_in % per_in) * span_in, span_in)
            for part, ks in zip(parts, plan.senders):

                @pl.when(among(source, ks))
                def _():
                    operand[...] = part[position(source, ks), :, pl.ds(place, span_in)]

            contract = (((1,), (1,)), ((), ())) if plan.forward else (((1,), (0,)), ((), ()))
            term = lax.dot_general(
                operand[...], tiles[slot], contract, preferred_element_type=jnp.float32
            )
            to = pl.multiple_of((block_out % per_out) * span_out, span_out)
            for total, out in zip(sums, plan.outs):

                @pl.when(among(target, out.ks))
                def _():
                    total[position(target, out.ks), :, pl.ds(to, span_out)] += term

        return carry

    lax.fori_loop(0, live[0, 0], visit, 0)
    for out, result, total in zip(plan.outs, results, sums):
        if not out.direct:
            each = len(out.ks) // len(result)
            for i, ref in enumerate(result):
                ref[...] = total[i * each : (i + 1) * each].astype(ref.dtype)


def sweep(plan, tiles, places, live, parts, begun, wide):
    slots, rows_tile, cols_tile = tiles.shape
    width = parts[0].shape[1]
    span_in = cols_tile if plan.forward else rows_tile
    plan = plan._replace(begun=bool(begun))
    out_shape = []
    scratch = [pltpu.VMEM((width, span_in), jnp.bfloat16)]
    for out in plan.outs:
        many = len(out.ks)
        if out.stacked:
            out_shape += [jax.ShapeDtypeStruct((many, width, wide), out.kind)]
        else:
            out_shape += [jax.ShapeDtypeStruct((1, width, wide), out.kind)] * many
        if not out.direct:
            scratch += [pltpu.VMEM((many, width, wide), jnp.float32)]
    vmem = pl.BlockSpec(memory_space=pltpu.VMEM)
    flat = pl.pallas_call(
        functools.partial(sweep_kernel, plan, parts[0].shape[2] // span_in),
        out_shape=out_shape,
        in_specs=[pl.BlockSpec(memory_space=pltpu.SMEM)] * 2
        + [vmem] * (1 + len(parts) + len(begun)),
        out_specs=[vmem] * len(out_shape),
        scratch_shapes=scratch,
        compiler_params=pltpu.CompilerParams(vmem_limit_bytes=VMEM_LIMIT),
        cost_estimate=pl.CostEstimate(
            flops=slots * width * rows_tile * cols_tile,
            bytes_accessed=tiles.size,
            transcendentals=0,
        ),
        name="forward_sweep" if plan.forward else "transpose_sweep",
    )(places, live, tiles, *parts, *begun)
    flat = list(flat)
    return [
        flat.pop(0) if out.stacked else {k: flat.pop(0) for k in out.ks} for out in plan.outs
    ]


def load_kernel(live, tiles, held, arrived):
    def fetch(slot):
        return pltpu.make_async_copy(tiles.at[slot], held.at[slot], arrived.at[slot])

    def start(slot, carry):
        fetch(slot).start()
        return carry

    def finish(slot, carry):
        fetch(slot).wait()
        return carry

    lax.fori_loop(0, live[0, 0], start, 0)
    lax.fori_loop(0, live[0, 0], finish, 0)


def load_tiles(live, tiles):
    return pl.pallas_call(
        load_kernel,
        out_shape=jax.ShapeDtypeStruct(tiles.shape, tiles.dtype),
        in_specs=[pl.BlockSpec(memory_space=pltpu.SMEM), pl.BlockSpec(memory_space=pl.ANY)],
        out_specs=pl.BlockSpec(memory_space=pltpu.VMEM),
        scratch_shapes=[pltpu.SemaphoreType.DMA((tiles.shape[0],))],
        compiler_params=pltpu.CompilerParams(vmem_limit_bytes=LOAD_LIMIT),
        cost_estimate=pl.CostEstimate(
            flops=0, bytes_accessed=4 * tiles.size, transcendentals=0
        ),
        name="load_tiles",
    )(live, tiles)


def swap(value, axis, size, k):
    return lax.ppermute(value, axis, [(i, i ^ k) for i in range(size)])


def strides(size):
    return sorted(range(2, size, 2), key=lambda k: (k % 4 != 0, k))


def gather_pairs(own, axis, size):
    parts = [None] * size
    parts[0] = own
    for k in strides(size):
        parts[k] = swap(own, axis, size, k)
    for k in [0] + strides(size):
        parts[k + 1] = swap(parts[k], axis, size, 1)
    return parts


def update_kernel(shares, last, *refs):
    parts, (own, demand, kind, dual), outs = refs[:shares], refs[shares : shares + 4], refs[shares + 4 :]
    push = own[0]
    for part in parts:
        push = push + part[0].astype(jnp.float32)
    moved = dual[...] + step_dual * (demand[...] - push)
    moved = jnp.where(kind[...] == 1, jnp.maximum(moved, 0.0), moved)
    if last:
        outs[0][:, 0, :] = moved
    else:
        outs[0][...] = moved
        outs[1][0] = moved.astype(outs[1].dtype)


def update_dual(parts, own, demand, kind, dual, last):
    width, span = dual.shape
    vmem = pl.BlockSpec(memory_space=pltpu.VMEM)
    if last:
        out_shape = [jax.ShapeDtypeStruct((width, 1, span), jnp.float32)]
    else:
        out_shape = [
            jax.ShapeDtypeStruct((width, span), jnp.float32),
            jax.ShapeDtypeStruct((1, width, span), jnp.bfloat16),
        ]
    return pl.pallas_call(
        functools.partial(update_kernel, len(parts), last),
        out_shape=out_shape,
        in_specs=[vmem] * (len(parts) + 4),
        out_specs=[vmem] * len(out_shape),
        compiler_params=pltpu.CompilerParams(vmem_limit_bytes=VMEM_LIMIT),
        cost_estimate=pl.CostEstimate(
            flops=width * span * 16, bytes_accessed=width * span * 16, transcendentals=0
        ),
        name="update_dual",
    )(*parts, own, demand, kind, dual)


def share_pairs(kept, sent, axis, size):
    shares = []
    for k in strides(size):
        pair = kept[k] + swap(sent[k + 1], axis, size, 1).astype(jnp.float32)
        shares.append(swap(pair.astype(jnp.bfloat16), axis, size, k))
    return shares + [swap(sent[1], axis, size, 1)]


def sum_halves(kept, sent, axis, size):
    here = kept + swap(sent, axis, size, 1).astype(jnp.float32)
    away = here.astype(jnp.bfloat16)
    total = here
    for t in range(1, size // 2):
        other = swap(away, axis, size, 2 * t)
        order = [h ^ t for h in range(size // 2)]
        total = total + jnp.stack([other[h] for h in order]).astype(jnp.float32)
    return total


def body(
    rows,
    cols,
    tiles,
    tile_index,
    tile_count,
    weights,
    carbon,
    completion,
    demand,
    row_kind,
    primal_start,
    dual_start,
):
    places = tile_index[0, 0].T
    dual = dual_start[:, 0, :]
    rounded_dual = [dual.astype(jnp.bfloat16)[None]]
    state = jnp.concatenate([primal_start[:, 0, :], carbon, completion])
    states = [state] + [swap(state, "row", rows, k) for k in range(2, rows, 2)]
    states = jnp.stack(states)
    width = weights.shape[0]
    primal = states[:, :width]
    share = weights[:, None]
    cost = share * states[:, width : width + 1] + (1.0 - share) * states[:, width + 1 :]
    whole, rounded = jnp.float32, jnp.bfloat16
    order = [k for pair in strides(cols)[::-1] + [0] for k in (pair + 1, pair)]
    mine, other = (tuple(range(p, rows, 2)) for p in (0, 1))
    blocks = load_tiles(tile_count, tiles[0, 0])
    keep = tuple(range(0, cols, 2))
    leave = [k + 1 for k in strides(cols) + [0]]
    first, then = tuple(leave[:2]), tuple(leave[2:])
    for step in range(ITERS):
        dual_parts = gather_pairs(rounded_dual[0], "col", cols)
        sent, kept = [
            sweep(
                Plan(
                    False, tuple((k,) for k in order),
                    (Out(other, rounded, True) if sending else Out(mine, whole, True),), False,
                ),
                blocks, places, tile_count, [dual_parts[k] for k in order], [], primal.shape[2],
            )[0]
            for sending in (True, False)
        ]
        pull = sum_halves(kept, sent, "row", rows)
        fresh = jnp.maximum(primal - step_primal * (cost - pull), 0.0)
        extra = (2.0 * fresh - primal).astype(jnp.bfloat16)
        primal = fresh
        extra = [extra, swap(extra, "row", rows, 1)]
        (sent,) = sweep(
            Plan(True, (mine, other), (Out(first, rounded, False),), False),
            blocks, places, tile_count, extra, [], dual.shape[1],
        )
        rest, kept = sweep(
            Plan(
                True, (mine, other),
                (Out(then, rounded, False), Out(keep, whole, False)), False,
            ),
            blocks, places, tile_count, extra, [], dual.shape[1],
        )
        sent |= rest
        shares = share_pairs(kept, sent, "col", cols)
        dual, *rounded_dual = update_dual(
            shares, kept[0], demand, row_kind, dual, step == ITERS - 1
        )
    return (primal[0][:, None, :], dual)


def solution(mesh):
    placed = (
        P("row", "col", None, None, None),
        P("row", "col", None, None),
        P("row", "col"),
        P(),
        P("col", "row"),
        P("col", "row"),
        P("row", "col"),
        P("row", "col"),
        P(None, "col", "row"),
        P(None, "row", "col"),
    )
    return jax.shard_map(
        functools.partial(body, mesh.shape["row"], mesh.shape["col"]),
        mesh=mesh,
        in_specs=placed,
        out_specs=(P(None, "col", "row"), P(None, "row", "col")),
        check_vma=False,
    )
```

```python
import functools
import typing

import jax
import jax.numpy as jnp
from jax import lax
from jax.experimental import pallas as pl
from jax.experimental.pallas import tpu as pltpu
from jax.sharding import PartitionSpec as P

BR_DEV = 16
BC_DEV = 16
ITERS = 2


step_primal = 0.4
step_dual = 0.4

VMEM_LIMIT = 24 * 1024 * 1024
LOAD_LIMIT = 42 * 1024 * 1024


def among(value, ks):
    return ((sum(1 << k for k in ks) >> value) & 1) == 1


def position(value, ks):
    at = 0
    for i, k in enumerate(ks[1:]):
        at = jnp.where(value == k, i + 1, at)
    return at


class Out(typing.NamedTuple):
    ks: tuple
    kind: typing.Any
    stacked: bool

    @property
    def direct(self):
        return self.kind == jnp.float32


class Plan(typing.NamedTuple):
    forward: bool
    senders: tuple
    outs: tuple


def sweep_kernel(plan, per_in, places, live, tiles, *refs):
    refs = list(refs)
    parts = [refs.pop(0) for _ in plan.senders]
    results = [[refs.pop(0) for _ in (out.ks[:1] if out.stacked else out.ks)] for out in plan.outs]
    operand = refs.pop(0)
    sums = [result if out.direct else [refs.pop(0)] for out, result in zip(plan.outs, results)]
    me_in = lax.axis_index("row" if plan.forward else "col")
    me_out = lax.axis_index("col" if plan.forward else "row")
    span_in = operand.shape[1]
    span_out = tiles.shape[1] if plan.forward else tiles.shape[2]
    per_out = sums[0][0].shape[2] // span_out

    def ends(slot):
        row, col = places[0, slot], places[1, slot]
        return (col, row) if plan.forward else (row, col)

    receivers = sum((out.ks for out in plan.outs), ())

    for total in sum(sums, []):
        total[...] = jnp.zeros_like(total)

    def visit(slot, carry):
        block_in, block_out = ends(slot)
        target = (block_out // per_out) ^ me_out

        @pl.when(among(target, receivers))
        def _():
            source = (block_in // per_in) ^ me_in
            place = pl.multiple_of((block_in % per_in) * span_in, span_in)
            for part, ks in zip(parts, plan.senders):

                @pl.when(among(source, ks))
                def _():
                    operand[...] = part[position(source, ks), :, pl.ds(place, span_in)]

            contract = (((1,), (1,)), ((), ())) if plan.forward else (((1,), (0,)), ((), ()))
            term = lax.dot_general(
                operand[...], tiles[slot], contract, preferred_element_type=jnp.float32
            )
            to = pl.multiple_of((block_out % per_out) * span_out, span_out)
            for totals, out in zip(sums, plan.outs):
                for total, ks in zip(totals, [out.ks] if len(totals) == 1 else [(k,) for k in out.ks]):

                    @pl.when(among(target, ks) if ks != receivers else True)
                    def _():
                        total[position(target, ks), :, pl.ds(to, span_out)] += term

        return carry

    lax.fori_loop(0, live[0, 0], visit, 0)
    for out, result, (total, *_) in zip(plan.outs, results, sums):
        if not out.direct:
            each = len(out.ks) // len(result)
            for i, ref in enumerate(result):
                ref[...] = total[i * each : (i + 1) * each].astype(ref.dtype)


def sweep(plan, tiles, places, live, parts, wide):
    slots, rows_tile, cols_tile = tiles.shape
    width = parts[0].shape[1]
    span_in = cols_tile if plan.forward else rows_tile
    out_shape = []
    scratch = [pltpu.VMEM((width, span_in), jnp.bfloat16)]
    for out in plan.outs:
        many = len(out.ks)
        if out.stacked:
            out_shape += [jax.ShapeDtypeStruct((many, width, wide), out.kind)]
        else:
            out_shape += [jax.ShapeDtypeStruct((1, width, wide), out.kind)] * many
        if not out.direct:
            scratch += [pltpu.VMEM((many, width, wide), jnp.float32)]
    vmem = pl.BlockSpec(memory_space=pltpu.VMEM)
    flat = pl.pallas_call(
        functools.partial(sweep_kernel, plan, parts[0].shape[2] // span_in),
        out_shape=out_shape,
        in_specs=[pl.BlockSpec(memory_space=pltpu.SMEM)] * 2
        + [vmem] * (1 + len(parts)),
        out_specs=[vmem] * len(out_shape),
        scratch_shapes=scratch,
        compiler_params=pltpu.CompilerParams(vmem_limit_bytes=VMEM_LIMIT),
        cost_estimate=pl.CostEstimate(
            flops=slots * width * rows_tile * cols_tile,
            bytes_accessed=tiles.size,
            transcendentals=0,
        ),
        name="forward_sweep" if plan.forward else "transpose_sweep",
    )(places, live, tiles, *parts)
    flat = list(flat)
    return [
        flat.pop(0) if out.stacked else {k: flat.pop(0) for k in out.ks} for out in plan.outs
    ]


def load_kernel(live, tiles, held, arrived):
    def fetch(slot):
        return pltpu.make_async_copy(tiles.at[slot], held.at[slot], arrived.at[slot])

    def start(slot, carry):
        fetch(slot).start()
        return carry

    def finish(slot, carry):
        fetch(slot).wait()
        return carry

    lax.fori_loop(0, live[0, 0], start, 0)
    lax.fori_loop(0, live[0, 0], finish, 0)


def load_tiles(live, tiles):
    return pl.pallas_call(
        load_kernel,
        out_shape=jax.ShapeDtypeStruct(tiles.shape, tiles.dtype),
        in_specs=[pl.BlockSpec(memory_space=pltpu.SMEM), pl.BlockSpec(memory_space=pl.ANY)],
        out_specs=pl.BlockSpec(memory_space=pltpu.VMEM),
        scratch_shapes=[pltpu.SemaphoreType.DMA((tiles.shape[0],))],
        compiler_params=pltpu.CompilerParams(vmem_limit_bytes=LOAD_LIMIT),
        cost_estimate=pl.CostEstimate(
            flops=0, bytes_accessed=4 * tiles.size, transcendentals=0
        ),
        name="load_tiles",
    )(live, tiles)


def swap(value, axis, size, k):
    return lax.ppermute(value, axis, [(i, i ^ k) for i in range(size)])


def strides(size):
    return sorted(range(2, size, 2), key=lambda k: (k % 4 != 0, k))


def gather_pairs(own, axis, size):
    parts = [None] * size
    parts[0] = own
    for k in strides(size):
        parts[k] = swap(own, axis, size, k)
    for k in [0] + strides(size):
        parts[k + 1] = swap(parts[k], axis, size, 1)
    return parts


def update_kernel(shares, last, *refs):
    parts, (own, demand, kind, dual), outs = refs[:shares], refs[shares : shares + 4], refs[shares + 4 :]
    push = own[0]
    for part in parts:
        push = push + part[0].astype(jnp.float32)
    moved = dual[...] + step_dual * (demand[...] - push)
    moved = jnp.where(kind[...] == 1, jnp.maximum(moved, 0.0), moved)
    if last:
        outs[0][:, 0, :] = moved
    else:
        outs[0][...] = moved
        outs[1][0] = moved.astype(outs[1].dtype)


def update_dual(parts, own, demand, kind, dual, last):
    width, span = dual.shape
    vmem = pl.BlockSpec(memory_space=pltpu.VMEM)
    if last:
        out_shape = [jax.ShapeDtypeStruct((width, 1, span), jnp.float32)]
    else:
        out_shape = [
            jax.ShapeDtypeStruct((width, span), jnp.float32),
            jax.ShapeDtypeStruct((1, width, span), jnp.bfloat16),
        ]
    return pl.pallas_call(
        functools.partial(update_kernel, len(parts), last),
        out_shape=out_shape,
        in_specs=[vmem] * (len(parts) + 4),
        out_specs=[vmem] * len(out_shape),
        compiler_params=pltpu.CompilerParams(vmem_limit_bytes=VMEM_LIMIT),
        cost_estimate=pl.CostEstimate(
            flops=width * span * 16, bytes_accessed=width * span * 16, transcendentals=0
        ),
        name="update_dual",
    )(*parts, own, demand, kind, dual)


def share_pairs(kept, sent, axis, size):
    shares = []
    for k in strides(size):
        pair = kept[k] + swap(sent[k + 1], axis, size, 1).astype(jnp.float32)
        shares.append(swap(pair.astype(jnp.bfloat16), axis, size, k))
    return shares + [swap(sent[1], axis, size, 1)]


def sum_halves(kept, sent, axis, size):
    here = kept + swap(sent, axis, size, 1).astype(jnp.float32)
    away = here.astype(jnp.bfloat16)
    total = here
    for t in range(1, size // 2):
        other = swap(away, axis, size, 2 * t)
        order = [h ^ t for h in range(size // 2)]
        total = total + jnp.stack([other[h] for h in order]).astype(jnp.float32)
    return total


def body(
    rows,
    cols,
    tiles,
    tile_index,
    tile_count,
    weights,
    carbon,
    completion,
    demand,
    row_kind,
    primal_start,
    dual_start,
):
    places = tile_index[0, 0].T
    dual = dual_start[:, 0, :]
    rounded_dual = [dual.astype(jnp.bfloat16)[None]]
    state = jnp.concatenate([primal_start[:, 0, :], carbon, completion])
    states = [state] + [swap(state, "row", rows, k) for k in range(2, rows, 2)]
    states = jnp.stack(states)
    width = weights.shape[0]
    primal = states[:, :width]
    share = weights[:, None]
    cost = share * states[:, width : width + 1] + (1.0 - share) * states[:, width + 1 :]
    whole, rounded = jnp.float32, jnp.bfloat16
    order = [k for pair in strides(cols)[::-1] + [0] for k in (pair + 1, pair)]
    mine, other = (tuple(range(p, rows, 2)) for p in (0, 1))
    blocks = load_tiles(tile_count, tiles[0, 0])
    keep = tuple(range(0, cols, 2))
    leave = [k + 1 for k in strides(cols) + [0]]
    first, then = tuple(leave[:2]), tuple(leave[2:])
    for step in range(ITERS):
        dual_parts = gather_pairs(rounded_dual[0], "col", cols)
        sent, kept = [
            sweep(
                Plan(
                    False, tuple((k,) for k in order),
                    (Out(other, rounded, True) if sending else Out(mine, whole, True),),
                ),
                blocks, places, tile_count, [dual_parts[k] for k in order], primal.shape[2],
            )[0]
            for sending in (True, False)
        ]
        pull = sum_halves(kept, sent, "row", rows)
        fresh = jnp.maximum(primal - step_primal * (cost - pull), 0.0)
        extra = (2.0 * fresh - primal).astype(jnp.bfloat16)
        primal = fresh
        extra = [extra, swap(extra, "row", rows, 1)]
        (sent,) = sweep(
            Plan(True, (mine, other), (Out(first, rounded, False),)),
            blocks, places, tile_count, extra, dual.shape[1],
        )
        rest, kept = sweep(
            Plan(
                True, (mine, other),
                (Out(then, rounded, False), Out(keep, whole, False)),
            ),
            blocks, places, tile_count, extra, dual.shape[1],
        )
        sent |= rest
        shares = share_pairs(kept, sent, "col", cols)
        dual, *rounded_dual = update_dual(
            shares, kept[0], demand, row_kind, dual, step == ITERS - 1
        )
    return (primal[0][:, None, :], dual)


def solution(mesh):
    placed = (
        P("row", "col", None, None, None),
        P("row", "col", None, None),
        P("row", "col"),
        P(),
        P("col", "row"),
        P("col", "row"),
        P("row", "col"),
        P("row", "col"),
        P(None, "col", "row"),
        P(None, "row", "col"),
    )
    return jax.shard_map(
        functools.partial(body, mesh.shape["row"], mesh.shape["col"]),
        mesh=mesh,
        in_specs=placed,
        out_specs=(P(None, "col", "row"), P(None, "row", "col")),
        check_vma=False,
    )
```

```python
import functools
import typing

import jax
import jax.numpy as jnp
from jax import lax
from jax.experimental import pallas as pl
from jax.experimental.pallas import tpu as pltpu
from jax.sharding import PartitionSpec as P

BR_DEV = 16
BC_DEV = 16
ITERS = 2


step_primal = 0.4
step_dual = 0.4

VMEM_LIMIT = 24 * 1024 * 1024
LOAD_LIMIT = 42 * 1024 * 1024


def among(value, ks):
    return ((sum(1 << k for k in ks) >> value) & 1) == 1


def position(value, ks):
    at = 0
    for i, k in enumerate(ks[1:]):
        at = jnp.where(value == k, i + 1, at)
    return at


class Out(typing.NamedTuple):
    ks: tuple
    kind: typing.Any
    stacked: bool

    @property
    def direct(self):
        return self.kind == jnp.float32


class Plan(typing.NamedTuple):
    forward: bool
    senders: tuple
    outs: tuple


def sweep_kernel(plan, per_in, block_rows, block_cols, live, tiles, *refs):
    refs = list(refs)
    parts = [refs.pop(0) for _ in plan.senders]
    results = [[refs.pop(0) for _ in (out.ks[:1] if out.stacked else out.ks)] for out in plan.outs]
    operand = refs.pop(0)
    sums = [result if out.direct else [refs.pop(0)] for out, result in zip(plan.outs, results)]
    me_in = lax.axis_index("row" if plan.forward else "col")
    me_out = lax.axis_index("col" if plan.forward else "row")
    span_in = operand.shape[1]
    span_out = tiles.shape[1] if plan.forward else tiles.shape[2]
    per_out = sums[0][0].shape[2] // span_out

    def ends(slot):
        row = (block_rows[0, 0] >> (4 * slot)) & 15
        col = (block_cols[0, 0] >> (4 * slot)) & 15
        return (col, row) if plan.forward else (row, col)

    receivers = sum((out.ks for out in plan.outs), ())

    for total in sum(sums, []):
        total[...] = jnp.zeros_like(total)

    def visit(slot, carry):
        block_in, block_out = ends(slot)
        target = (block_out // per_out) ^ me_out

        @pl.when(among(target, receivers))
        def _():
            source = (block_in // per_in) ^ me_in
            place = pl.multiple_of((block_in % per_in) * span_in, span_in)
            for part, ks in zip(parts, plan.senders):

                @pl.when(among(source, ks))
                def _():
                    operand[...] = part[position(source, ks), :, pl.ds(place, span_in)]

            contract = (((1,), (1,)), ((), ())) if plan.forward else (((1,), (0,)), ((), ()))
            term = lax.dot_general(
                operand[...], tiles[slot], contract, preferred_element_type=jnp.float32
            )
            to = pl.multiple_of((block_out % per_out) * span_out, span_out)
            for totals, out in zip(sums, plan.outs):
                for total, ks in zip(totals, [out.ks] if len(totals) == 1 else [(k,) for k in out.ks]):

                    @pl.when(among(target, ks) if ks != receivers else True)
                    def _():
                        total[position(target, ks), :, pl.ds(to, span_out)] += term

        return carry

    lax.fori_loop(0, live[0, 0], visit, 0)
    for out, result, (total, *_) in zip(plan.outs, results, sums):
        if not out.direct:
            each = len(out.ks) // len(result)
            for i, ref in enumerate(result):
                ref[...] = total[i * each : (i + 1) * each].astype(ref.dtype)


def sweep(plan, tiles, places, parts, wide):
    slots, rows_tile, cols_tile = tiles.shape
    width = parts[0].shape[1]
    span_in = cols_tile if plan.forward else rows_tile
    out_shape = []
    scratch = [pltpu.VMEM((width, span_in), jnp.bfloat16)]
    for out in plan.outs:
        many = len(out.ks)
        if out.stacked:
            out_shape += [jax.ShapeDtypeStruct((many, width, wide), out.kind)]
        else:
            out_shape += [jax.ShapeDtypeStruct((1, width, wide), out.kind)] * many
        if not out.direct:
            scratch += [pltpu.VMEM((many, width, wide), jnp.float32)]
    vmem = pl.BlockSpec(memory_space=pltpu.VMEM)
    flat = pl.pallas_call(
        functools.partial(sweep_kernel, plan, parts[0].shape[2] // span_in),
        out_shape=out_shape,
        in_specs=[pl.BlockSpec(memory_space=pltpu.SMEM)] * 3
        + [vmem] * (1 + len(parts)),
        out_specs=[vmem] * len(out_shape),
        scratch_shapes=scratch,
        compiler_params=pltpu.CompilerParams(vmem_limit_bytes=VMEM_LIMIT),
        cost_estimate=pl.CostEstimate(
            flops=slots * width * rows_tile * cols_tile,
            bytes_accessed=tiles.size,
            transcendentals=0,
        ),
        name="forward_sweep" if plan.forward else "transpose_sweep",
    )(*places, tiles, *parts)
    flat = list(flat)
    return [
        flat.pop(0) if out.stacked else {k: flat.pop(0) for k in out.ks} for out in plan.outs
    ]


def load_kernel(live, tiles, held, arrived):
    def fetch(slot):
        return pltpu.make_async_copy(tiles.at[slot], held.at[slot], arrived.at[slot])

    def start(slot, carry):
        fetch(slot).start()
        return carry

    def finish(slot, carry):
        fetch(slot).wait()
        return carry

    lax.fori_loop(0, live[0, 0], start, 0)
    lax.fori_loop(0, live[0, 0], finish, 0)


def load_tiles(live, tiles):
    return pl.pallas_call(
        load_kernel,
        out_shape=jax.ShapeDtypeStruct(tiles.shape, tiles.dtype),
        in_specs=[pl.BlockSpec(memory_space=pltpu.SMEM), pl.BlockSpec(memory_space=pl.ANY)],
        out_specs=pl.BlockSpec(memory_space=pltpu.VMEM),
        scratch_shapes=[pltpu.SemaphoreType.DMA((tiles.shape[0],))],
        compiler_params=pltpu.CompilerParams(vmem_limit_bytes=LOAD_LIMIT),
        cost_estimate=pl.CostEstimate(
            flops=0, bytes_accessed=4 * tiles.size, transcendentals=0
        ),
        name="load_tiles",
    )(live, tiles)


def swap(value, axis, size, k):
    return lax.ppermute(value, axis, [(i, i ^ k) for i in range(size)])


def strides(size):
    return sorted(range(2, size, 2), key=lambda k: (k % 4 != 0, k))


def gather_pairs(own, axis, size):
    parts = [None] * size
    parts[0] = own
    for k in strides(size):
        parts[k] = swap(own, axis, size, k)
    for k in [0] + strides(size):
        parts[k + 1] = swap(parts[k], axis, size, 1)
    return parts


def update_kernel(shares, last, *refs):
    parts, (own, demand, kind, dual), outs = refs[:shares], refs[shares : shares + 4], refs[shares + 4 :]
    push = own[0]
    for part in parts:
        push = push + part[0].astype(jnp.float32)
    moved = dual[...] + step_dual * (demand[...] - push)
    moved = jnp.where(kind[...] == 1, jnp.maximum(moved, 0.0), moved)
    if last:
        outs[0][:, 0, :] = moved
    else:
        outs[0][...] = moved
        outs[1][0] = moved.astype(outs[1].dtype)


def update_dual(parts, own, demand, kind, dual, last):
    width, span = dual.shape
    vmem = pl.BlockSpec(memory_space=pltpu.VMEM)
    if last:
        out_shape = [jax.ShapeDtypeStruct((width, 1, span), jnp.float32)]
    else:
        out_shape = [
            jax.ShapeDtypeStruct((width, span), jnp.float32),
            jax.ShapeDtypeStruct((1, width, span), jnp.bfloat16),
        ]
    return pl.pallas_call(
        functools.partial(update_kernel, len(parts), last),
        out_shape=out_shape,
        in_specs=[vmem] * (len(parts) + 4),
        out_specs=[vmem] * len(out_shape),
        compiler_params=pltpu.CompilerParams(vmem_limit_bytes=VMEM_LIMIT),
        cost_estimate=pl.CostEstimate(
            flops=width * span * 16, bytes_accessed=width * span * 16, transcendentals=0
        ),
        name="update_dual",
    )(*parts, own, demand, kind, dual)


def share_pairs(kept, sent, axis, size):
    shares = []
    for k in strides(size):
        pair = kept[k] + swap(sent[k + 1], axis, size, 1).astype(jnp.float32)
        shares.append(swap(pair.astype(jnp.bfloat16), axis, size, k))
    return shares + [swap(sent[1], axis, size, 1)]


def sum_halves(kept, sent, axis, size):
    here = kept + swap(sent, axis, size, 1).astype(jnp.float32)
    away = here.astype(jnp.bfloat16)
    total = here
    for t in range(1, size // 2):
        other = swap(away, axis, size, 2 * t)
        order = [h ^ t for h in range(size // 2)]
        total = total + jnp.stack([other[h] for h in order]).astype(jnp.float32)
    return total


def body(
    rows,
    cols,
    tiles,
    tile_index,
    tile_count,
    weights,
    carbon,
    completion,
    demand,
    row_kind,
    primal_start,
    dual_start,
):
    shifts = 4 * jnp.arange(tile_index.shape[2], dtype=jnp.int32)
    packed = jnp.sum(tile_index[0, 0] << shifts[:, None], axis=0, dtype=jnp.int32)
    none = lax.axis_index("col") // cols
    places = ((packed[0] | none).reshape(1, 1), (packed[1] | none).reshape(1, 1), tile_count)
    dual = dual_start[:, 0, :]
    rounded_dual = [dual.astype(jnp.bfloat16)[None]]
    state = jnp.concatenate([primal_start[:, 0, :], carbon, completion])
    states = [state] + [swap(state, "row", rows, k) for k in range(2, rows, 2)]
    states = jnp.stack(states)
    width = weights.shape[0]
    primal = states[:, :width]
    share = weights[:, None]
    cost = share * states[:, width : width + 1] + (1.0 - share) * states[:, width + 1 :]
    whole, rounded = jnp.float32, jnp.bfloat16
    order = [k for pair in strides(cols)[::-1] + [0] for k in (pair + 1, pair)]
    mine, other = (tuple(range(p, rows, 2)) for p in (0, 1))
    blocks = load_tiles(tile_count, tiles[0, 0])
    keep = tuple(range(0, cols, 2))
    leave = [k + 1 for k in strides(cols) + [0]]
    first, then = tuple(leave[:2]), tuple(leave[2:])
    for step in range(ITERS):
        dual_parts = gather_pairs(rounded_dual[0], "col", cols)
        sent, kept = [
            sweep(
                Plan(
                    False, tuple((k,) for k in order),
                    (Out(other, rounded, True) if sending else Out(mine, whole, True),),
                ),
                blocks, places, [dual_parts[k] for k in order], primal.shape[2],
            )[0]
            for sending in (True, False)
        ]
        pull = sum_halves(kept, sent, "row", rows)
        fresh = jnp.maximum(primal - step_primal * (cost - pull), 0.0)
        extra = (2.0 * fresh - primal).astype(jnp.bfloat16)
        primal = fresh
        extra = [extra, swap(extra, "row", rows, 1)]
        (sent,) = sweep(
            Plan(True, (mine, other), (Out(first, rounded, False),)),
            blocks, places, extra, dual.shape[1],
        )
        rest, kept = sweep(
            Plan(
                True, (mine, other),
                (Out(then, rounded, False), Out(keep, whole, False)),
            ),
            blocks, places, extra, dual.shape[1],
        )
        sent |= rest
        shares = share_pairs(kept, sent, "col", cols)
        dual, *rounded_dual = update_dual(
            shares, kept[0], demand, row_kind, dual, step == ITERS - 1
        )
    return (primal[0][:, None, :], dual)


def solution(mesh):
    placed = (
        P("row", "col", None, None, None),
        P("row", "col", None, None),
        P("row", "col"),
        P(),
        P("col", "row"),
        P("col", "row"),
        P("row", "col"),
        P("row", "col"),
        P(None, "col", "row"),
        P(None, "row", "col"),
    )
    return jax.shard_map(
        functools.partial(body, mesh.shape["row"], mesh.shape["col"]),
        mesh=mesh,
        in_specs=placed,
        out_specs=(P(None, "col", "row"), P(None, "row", "col")),
        check_vma=False,
    )
```

```python
import functools
import typing

import jax
import jax.numpy as jnp
from jax import lax
from jax.experimental import pallas as pl
from jax.experimental.pallas import tpu as pltpu
from jax.sharding import PartitionSpec as P

BR_DEV = 16
BC_DEV = 16
ITERS = 2


step_primal = 0.4
step_dual = 0.4

VMEM_LIMIT = 24 * 1024 * 1024
LOAD_LIMIT = 42 * 1024 * 1024


def among(value, ks):
    return ((sum(1 << k for k in ks) >> value) & 1) == 1


def position(value, ks):
    at = 0
    for i, k in enumerate(ks[1:]):
        at = jnp.where(value == k, i + 1, at)
    return at


class Out(typing.NamedTuple):
    ks: tuple
    kind: typing.Any
    stacked: bool

    @property
    def direct(self):
        return self.kind == jnp.float32


class Plan(typing.NamedTuple):
    forward: bool
    senders: tuple
    outs: tuple


def sweep_kernel(plan, per_in, block_rows, block_cols, live, tiles, *refs):
    refs = list(refs)
    parts = [refs.pop(0) for _ in plan.senders]
    results = [[refs.pop(0) for _ in (out.ks[:1] if out.stacked else out.ks)] for out in plan.outs]
    operand = refs.pop(0)
    sums = [result if out.direct else [refs.pop(0)] for out, result in zip(plan.outs, results)]
    me_in = lax.axis_index("row" if plan.forward else "col")
    me_out = lax.axis_index("col" if plan.forward else "row")
    span_in = operand.shape[1]
    span_out = tiles.shape[1] if plan.forward else tiles.shape[2]
    per_out = sums[0][0].shape[2] // span_out

    def ends(slot):
        row = (block_rows[0, 0] >> (4 * slot)) & 15
        col = (block_cols[0, 0] >> (4 * slot)) & 15
        return (col, row) if plan.forward else (row, col)

    receivers = sum((out.ks for out in plan.outs), ())

    for total in sum(sums, []):
        total[...] = jnp.zeros_like(total)

    def visit(slot, carry):
        block_in, block_out = ends(slot)
        target = (block_out // per_out) ^ me_out

        @pl.when(among(target, receivers))
        def _():
            source = (block_in // per_in) ^ me_in
            place = pl.multiple_of((block_in % per_in) * span_in, span_in)
            for part, ks in zip(parts, plan.senders):

                @pl.when(among(source, ks))
                def _():
                    operand[...] = part[position(source, ks), :, pl.ds(place, span_in)]

            contract = (((1,), (1,)), ((), ())) if plan.forward else (((1,), (0,)), ((), ()))
            term = lax.dot_general(
                operand[...], tiles[slot], contract, preferred_element_type=jnp.float32
            )
            to = pl.multiple_of((block_out % per_out) * span_out, span_out)
            for totals, out in zip(sums, plan.outs):
                for total, ks in zip(totals, [out.ks] if len(totals) == 1 else [(k,) for k in out.ks]):

                    @pl.when(among(target, ks) if ks != receivers else True)
                    def _():
                        total[position(target, ks), :, pl.ds(to, span_out)] += term

        return carry

    lax.fori_loop(0, live[0, 0], visit, 0)
    for out, result, (total, *_) in zip(plan.outs, results, sums):
        if not out.direct:
            each = len(out.ks) // len(result)
            for i, ref in enumerate(result):
                ref[...] = total[i * each : (i + 1) * each].astype(ref.dtype)


def sweep(plan, tiles, places, parts, wide):
    slots, rows_tile, cols_tile = tiles.shape
    width = parts[0].shape[1]
    span_in = cols_tile if plan.forward else rows_tile
    out_shape = []
    scratch = [pltpu.VMEM((width, span_in), jnp.bfloat16)]
    for out in plan.outs:
        many = len(out.ks)
        if out.stacked:
            out_shape += [jax.ShapeDtypeStruct((many, width, wide), out.kind)]
        else:
            out_shape += [jax.ShapeDtypeStruct((1, width, wide), out.kind)] * many
        if not out.direct:
            scratch += [pltpu.VMEM((many, width, wide), jnp.float32)]
    vmem = pl.BlockSpec(memory_space=pltpu.VMEM)
    flat = pl.pallas_call(
        functools.partial(sweep_kernel, plan, parts[0].shape[2] // span_in),
        out_shape=out_shape,
        in_specs=[pl.BlockSpec(memory_space=pltpu.SMEM)] * 3
        + [vmem] * (1 + len(parts)),
        out_specs=[vmem] * len(out_shape),
        scratch_shapes=scratch,
        compiler_params=pltpu.CompilerParams(vmem_limit_bytes=VMEM_LIMIT),
        cost_estimate=pl.CostEstimate(
            flops=slots * width * rows_tile * cols_tile,
            bytes_accessed=tiles.size,
            transcendentals=0,
        ),
        name="forward_sweep" if plan.forward else "transpose_sweep",
    )(*places, tiles, *parts)
    flat = list(flat)
    return [
        flat.pop(0) if out.stacked else {k: flat.pop(0) for k in out.ks} for out in plan.outs
    ]


def load_kernel(live, tiles, held, arrived):
    def fetch(slot):
        return pltpu.make_async_copy(tiles.at[slot], held.at[slot], arrived.at[slot])

    def start(slot, carry):
        fetch(slot).start()
        return carry

    def finish(slot, carry):
        fetch(slot).wait()
        return carry

    lax.fori_loop(0, live[0, 0], start, 0)
    lax.fori_loop(0, live[0, 0], finish, 0)


def load_tiles(live, tiles):
    return pl.pallas_call(
        load_kernel,
        out_shape=jax.ShapeDtypeStruct(tiles.shape, tiles.dtype),
        in_specs=[pl.BlockSpec(memory_space=pltpu.SMEM), pl.BlockSpec(memory_space=pl.ANY)],
        out_specs=pl.BlockSpec(memory_space=pltpu.VMEM),
        scratch_shapes=[pltpu.SemaphoreType.DMA((tiles.shape[0],))],
        compiler_params=pltpu.CompilerParams(vmem_limit_bytes=LOAD_LIMIT),
        cost_estimate=pl.CostEstimate(
            flops=0, bytes_accessed=4 * tiles.size, transcendentals=0
        ),
        name="load_tiles",
    )(live, tiles)


def swap(value, axis, size, k):
    return lax.ppermute(value, axis, [(i, i ^ k) for i in range(size)])


def strides(size):
    return sorted(range(2, size, 2), key=lambda k: (k % 4 != 0, k))


def gather_pairs(own, axis, size):
    parts = [None] * size
    parts[0] = own
    for k in strides(size):
        parts[k] = swap(own, axis, size, k)
    for k in [0] + strides(size):
        parts[k + 1] = swap(parts[k], axis, size, 1)
    return parts


def update_kernel(shares, last, *refs):
    parts, (own, demand, kind, dual), outs = refs[:shares], refs[shares : shares + 4], refs[shares + 4 :]
    push = own[0]
    for part in parts:
        push = push + part[0].astype(jnp.float32)
    moved = dual[...] + step_dual * (demand[...] - push)
    moved = jnp.where(kind[...] == 1, jnp.maximum(moved, 0.0), moved)
    if last:
        outs[0][:, 0, :] = moved
    else:
        outs[0][...] = moved
        outs[1][0] = moved.astype(outs[1].dtype)


def update_dual(parts, own, demand, kind, dual, last):
    width, span = dual.shape
    vmem = pl.BlockSpec(memory_space=pltpu.VMEM)
    if last:
        out_shape = [jax.ShapeDtypeStruct((width, 1, span), jnp.float32)]
    else:
        out_shape = [
            jax.ShapeDtypeStruct((width, span), jnp.float32),
            jax.ShapeDtypeStruct((1, width, span), jnp.bfloat16),
        ]
    return pl.pallas_call(
        functools.partial(update_kernel, len(parts), last),
        out_shape=out_shape,
        in_specs=[vmem] * (len(parts) + 4),
        out_specs=[vmem] * len(out_shape),
        compiler_params=pltpu.CompilerParams(vmem_limit_bytes=VMEM_LIMIT),
        cost_estimate=pl.CostEstimate(
            flops=width * span * 16, bytes_accessed=width * span * 16, transcendentals=0
        ),
        name="update_dual",
    )(*parts, own, demand, kind, dual)


def share_pairs(kept, sent, axis, size):
    shares = []
    for k in strides(size):
        pair = kept[k] + swap(sent[k + 1], axis, size, 1).astype(jnp.float32)
        shares.append(swap(pair.astype(jnp.bfloat16), axis, size, k))
    return shares + [swap(sent[1], axis, size, 1)]


def sum_halves(kept, sent, axis, size):
    here = kept + swap(sent, axis, size, 1).astype(jnp.float32)
    away = here.astype(jnp.bfloat16)
    total = here
    for t in range(1, size // 2):
        other = swap(away, axis, size, 2 * t)
        order = [h ^ t for h in range(size // 2)]
        total = total + jnp.stack([other[h] for h in order]).astype(jnp.float32)
    return total


def body(
    rows,
    cols,
    tiles,
    tile_index,
    tile_count,
    weights,
    carbon,
    completion,
    demand,
    row_kind,
    primal_start,
    dual_start,
):
    shifts = 4 * jnp.arange(tile_index.shape[2], dtype=jnp.int32)
    packed = jnp.sum(tile_index[0, 0] << shifts[:, None], axis=0, dtype=jnp.int32)
    none = lax.axis_index("col") // cols
    places = ((packed[0] | none).reshape(1, 1), (packed[1] | none).reshape(1, 1), tile_count)
    dual = dual_start[:, 0, :]
    rounded_dual = [dual.astype(jnp.bfloat16)[None]]
    state = jnp.concatenate([primal_start[:, 0, :], carbon, completion])
    states = [state] + [swap(state, "row", rows, k) for k in range(2, rows, 2)]
    states = jnp.stack(states)
    width = weights.shape[0]
    primal = states[:, :width]
    share = weights[:, None]
    cost = share * states[:, width : width + 1] + (1.0 - share) * states[:, width + 1 :]
    whole, rounded = jnp.float32, jnp.bfloat16
    order = [k for pair in strides(cols)[::-1] + [0] for k in (pair + 1, pair)]
    mine, other = (tuple(range(p, rows, 2)) for p in (0, 1))
    blocks = load_tiles(tile_count, tiles[0, 0])
    keep = tuple(range(0, cols, 2))
    soon = tuple(strides(cols)[:2])
    later = tuple(k for k in keep if k not in soon)
    leave = [k + 1 for k in strides(cols) + [0]]
    first, then = tuple(leave[:2]), tuple(leave[2:])
    for step in range(ITERS):
        dual_parts = gather_pairs(rounded_dual[0], "col", cols)
        sent, kept = [
            sweep(
                Plan(
                    False, tuple((k,) for k in order),
                    (Out(other, rounded, True) if sending else Out(mine, whole, True),),
                ),
                blocks, places, [dual_parts[k] for k in order], primal.shape[2],
            )[0]
            for sending in (True, False)
        ]
        pull = sum_halves(kept, sent, "row", rows)
        fresh = jnp.maximum(primal - step_primal * (cost - pull), 0.0)
        extra = (2.0 * fresh - primal).astype(jnp.bfloat16)
        primal = fresh
        extra = [extra, swap(extra, "row", rows, 1)]
        (sent,) = sweep(
            Plan(True, (mine, other), (Out(first, rounded, False),)),
            blocks, places, extra, dual.shape[1],
        )
        rest, kept = sweep(
            Plan(
                True, (mine, other),
                (Out(then, rounded, False), Out(soon, whole, False)),
            ),
            blocks, places, extra, dual.shape[1],
        )
        (last,) = sweep(
            Plan(True, (mine, other), (Out(later, whole, False),)),
            blocks, places, extra, dual.shape[1],
        )
        sent |= rest
        kept |= last
        shares = share_pairs(kept, sent, "col", cols)
        dual, *rounded_dual = update_dual(
            shares, kept[0], demand, row_kind, dual, step == ITERS - 1
        )
    return (primal[0][:, None, :], dual)


def solution(mesh):
    placed = (
        P("row", "col", None, None, None),
        P("row", "col", None, None),
        P("row", "col"),
        P(),
        P("col", "row"),
        P("col", "row"),
        P("row", "col"),
        P("row", "col"),
        P(None, "col", "row"),
        P(None, "row", "col"),
    )
    return jax.shard_map(
        functools.partial(body, mesh.shape["row"], mesh.shape["col"]),
        mesh=mesh,
        in_specs=placed,
        out_specs=(P(None, "col", "row"), P(None, "row", "col")),
        check_vma=False,
    )
```
